512 devices in a mesh: domain: 64 (over z_lo, y, core), band: 8 (over x, z_hi).
Axes of the slice: x: 4, y: 4, z: 16 (z_hi: 2, z_lo: 8; z = z_hi * 8 + z_lo), core: 2. Of those that a mesh axis runs over, the one named last changes fastest.
Arguments:
- states: float32 [110592, 1024], P('domain', 'band'), may hold values from -6 to 6
- connectivity: int32 [512, 343], P('domain'), may hold values from 0 to 2303, as said below
- cell_hamiltonian: float32 [512, 343, 343], P(('domain', 'band')), as said below
Outputs:
- filtered: float32 [110592, 1024], P('domain', 'band')
The draws below stay inside these ranges and needn't reach their ends.
Inputs may be any that keep to these rules, and one draw needn't show every extreme that they name: `connectivity`: each cell names 343 distinct positions of its subdomain's extended list of 2304 nodes. `cell_hamiltonian`: each matrix is symmetric.
All inputs are finite; a program needn't handle non-finite values.
Results may differ from the reference program's by a relative error of at most 0.0001.
Values sent between devices are 32-bit elements; how exact they have to be, the bound alone decides.
A program may use at most 64 MiB of HBM per device.

```python
import math
import jax
import jax.numpy as jnp
from jax import lax

NPC = 343
CELL_DEV = 8
NODE_DEV = 1728
FACE = 288
STATES = 1024
CELLS = 512
NODES = 110592
N_DOMAIN = 64


def draw_connectivity(key, part):
    key = jax.random.fold_in(key, 5)
    keys = jax.random.split(key, CELLS)
    extended = NODE_DEV + 2 * FACE

    def pick(single):
        return jax.random.permutation(single, extended)[:NPC]
    return jax.vmap(pick)(keys).astype(jnp.int32)


def draw_cell_hamiltonian(key, part):
    key = jax.random.fold_in(key, 11)
    first_key, second_key = jax.random.split(key)
    noise = jax.random.normal(first_key, (CELLS, NPC, NPC), jnp.float32)
    diagonal = jnp.exp(jax.random.uniform(second_key, (CELLS, NPC), jnp.float32, math.log(0.5), math.log(2.0)))
    symmetric = (noise + jnp.swapaxes(noise, 1, 2)) * (0.7071 / math.sqrt(NPC))
    identity = jnp.eye(NPC, dtype=jnp.float32)
    return symmetric + diagonal[:, :, None] * identity[None, :, :]


def block_scale(key, shape, cuts, low, top_value):
    gain = 1.0
    for dim, blocks in cuts:
        heights = jax.random.uniform(jax.random.fold_in(jax.random.fold_in(key, 6), dim), (blocks,), jnp.float32, low / len(cuts), top_value / len(cuts))
        gain = gain * jnp.repeat(jnp.exp(heights), shape[dim] // blocks).reshape((-1,) + (1,) * (len(shape) - 1 - dim))
    return gain


def centred(own_key, shape, deviation, bound, cuts=(), kind=jnp.bfloat16):
    values = jax.random.normal(own_key, shape, jnp.float32) * deviation
    if len(cuts) > 0:
        values = block_scale(own_key, shape, cuts, -0.22, 0.18) * values
    return jnp.clip(values, min=-bound, max=bound).astype(kind)


def setup_inputs(seed: int = 0) -> dict:
    key_list = jax.random.split(jax.random.key(seed), 4)
    return {
        "states": centred(key_list[0], (NODES, STATES), 1.0, 6.0, ((0, 64), (1, 8)), jnp.float32),
        "connectivity": draw_connectivity(jax.random.fold_in(key_list[3], 71), 0),
        "cell_hamiltonian": draw_cell_hamiltonian(jax.random.fold_in(key_list[3], 71), 0),
    }


filter_center = 0.5
filter_half = 1.5


def apply_hamiltonian(field, connectivity, cell_hamiltonian):
    padded = jnp.pad(field, ((FACE, FACE), (0, 0)))
    offsets = (jnp.arange(N_DOMAIN, dtype=jnp.int32) * NODE_DEV).astype(jnp.int32)
    links = connectivity.reshape(N_DOMAIN, CELL_DEV, NPC).astype(jnp.int32) + offsets[:, None, None]
    blocks = cell_hamiltonian.reshape(N_DOMAIN, CELL_DEV, NPC, NPC)

    def visit(total, item):
        link_block, cell_block = item
        picked = padded[link_block]
        prods = jnp.einsum("cij,cjs->cis", cell_block, picked, precision=lax.Precision.HIGHEST)
        total = total.at[link_block.reshape(-1)].add(prods.reshape(-1, field.shape[1]))
        return total, None

    total, _ = lax.scan(visit, jnp.zeros_like(padded), (links, blocks))
    return total[FACE:FACE + NODES]


def reference(states, connectivity, cell_hamiltonian):
    applied = apply_hamiltonian(states, connectivity, cell_hamiltonian)
    first = (applied - filter_center * states) / filter_half
    second = apply_hamiltonian(first, connectivity, cell_hamiltonian)
    return 2.0 * (second - filter_center * first) / filter_half - states
```

```python
import functools

import jax
import jax.numpy as jnp
from jax import lax
from jax.experimental import pallas as pl
from jax.experimental.pallas import tpu as pltpu
from jax.sharding import PartitionSpec as P

MESH = pl.DeviceIdType.MESH
f32, bf16, i32, i16 = jnp.float32, jnp.bfloat16, jnp.int32, jnp.int16

NPC = 343
KC = 352
CELLS = 8
FACE = 288
OWN = 1728
EXT = OWN + 2 * FACE
COLS = 128
INNER = OWN - 2 * FACE

LOW = INNER
HIGH = INNER + 2 * FACE
EARLY = 1024

PB, PA, PD, PC, PROWS = 0, 176, 304, 432, 520
PIECES = ((PB, 176), (PA, 128), (PD, 128), (PC, 88))

center = 0.5
half = 1.5


def split(value):
    hi = value.astype(bf16)
    lo = (value - hi.astype(f32)).astype(bf16)
    return hi, lo


def kernel(
    states, conn, cell, out,
    G, S, Hs, X, PR, E, RX, T, SX, F, XR, YR, Hf, CP, CR,
    z_send, x_send, f_send, n_send, cell_recv, n_recv,
):
    d = lax.axis_index("domain")
    b = lax.axis_index("band")
    last = lax.axis_size("domain") - 1
    nx = CELLS // 2
    xi = b // 2
    zh = b % 2
    zpeer = 2 * xi + 1 - zh
    xpeers = [2 * ((xi + j) % nx) + zh for j in (1, 3, 2)]
    has_low = d > 0
    has_high = d < last

    barrier = pltpu.get_barrier_semaphore()

    def greet(dd, bb):
        pl.semaphore_signal(barrier, inc=1, device_id=(dd, bb), device_id_type=MESH)

    greet(d, zpeer)
    for p in xpeers:
        greet(d, p)

    @pl.when(has_low)
    def _():
        greet(d - 1, b)

    @pl.when(has_high)
    def _():
        greet(d + 1, b)

    Hf[...] = jnp.zeros_like(Hf)
    Hf[0:NPC, 0:NPC] = cell[0]
    row = lax.broadcasted_iota(i32, (128, 128), 0)
    col = lax.broadcasted_iota(i32, (128, 128), 1)
    row88 = lax.broadcasted_iota(i32, (88, 128), 0)
    d2 = Hf[128:256, 128:256]
    diag = jnp.sum(jnp.where(row == col, d2, 0.0), axis=0, keepdims=True)
    RX[b, PB : PB + 88] = jnp.where(row88 == 87, diag, Hf[256:344, 0:128])
    RX[b, PB + 88 : PB + 176] = Hf[256:344, 128:256]
    RX[b, PA : PA + 128] = Hf[128:256, 0:128]
    RX[b, PD : PD + 128] = jnp.where(row >= col, Hf[0:128, 0:128], d2)
    RX[b, PC : PC + 88] = Hf[256:344, 256:384]

    pl.semaphore_wait(barrier, 4 + has_low.astype(i32) + has_high.astype(i32))

    def piece_copy(e, k, target, send_sem):
        at, rows = PIECES[k]
        part = RX.at[e, pl.ds(at, rows)]
        return pltpu.make_async_remote_copy(
            src_ref=part, dst_ref=part, send_sem=send_sem, recv_sem=cell_recv.at[e, k],
            device_id=(d, target), device_id_type=MESH,
        )

    def whole_copy(e, target, send_sem):
        return pltpu.make_async_remote_copy(
            src_ref=RX.at[e], dst_ref=RX.at[e], send_sem=send_sem, recv_sem=cell_recv.at[e, 0],
            device_id=(d, target), device_id_type=MESH,
        )

    def node_copy(src, dst, i, dd):
        return pltpu.make_async_remote_copy(
            src_ref=src, dst_ref=dst, send_sem=n_send.at[i], recv_sem=n_recv.at[i],
            device_id=(dd, b), device_id_type=MESH,
        )

    z_copies = [piece_copy(b, k, zpeer, z_send.at[k]) for k in range(4)]
    for c in z_copies:
        c.start()
    x_copies = [whole_copy(b, p, x_send.at[j]) for j, p in enumerate(xpeers)]
    for c in x_copies:
        c.start()

    def exchange(step, down_src, down_dst, up_src, up_dst):
        down = node_copy(down_src, down_dst, 2 * step, d - 1)
        up = node_copy(up_src, up_dst, 2 * step + 1, d + 1)
        return down, up

    halo_down, halo_up = exchange(
        0, states.at[pl.ds(0, FACE)], SX.at[pl.ds(HIGH + FACE, FACE)],
        states.at[pl.ds(OWN - FACE, FACE)], SX.at[pl.ds(LOW, FACE)],
    )
    sum_down, sum_up = exchange(
        1, T.at[pl.ds(LOW, 2 * FACE)], XR.at[1], T.at[pl.ds(HIGH, 2 * FACE)], XR.at[0]
    )
    own_down, own_up = exchange(
        2, T.at[pl.ds(LOW, FACE)], YR.at[1], T.at[pl.ds(HIGH + FACE, FACE)], YR.at[0]
    )

    @pl.when(has_low)
    def _():
        halo_down.start()

    @pl.when(has_high)
    def _():
        halo_up.start()

    CP[...] = jnp.full(CP.shape, -1, i32)
    n = conn[...]
    CP[:, 0:NPC] = jnp.where(n < 2 * FACE, n + LOW, jnp.where(n < OWN, n - 2 * FACE, n))

    def cell_of(s):
        side = s // nx
        return 2 * ((xi + s) % nx) + zh + side * (1 - 2 * zh)

    rows = [CP[pl.ds(cell_of(s), 1), :] for s in range(CELLS)]
    near = [r[:, :KC] for r in rows[:nx]]
    top = [r[:, :256] for r in rows[nx:]]
    bottom = [r[:, 256:KC] for r in rows[nx:]]
    CR[...] = jnp.concatenate(near + top + bottom, axis=1)

    def build_g(s, carry):
        line = jnp.broadcast_to(CP[pl.ds(cell_of(s), 1), :], (8, 384))
        column = jnp.transpose(line)[:KC, 0:1]
        wanted = jnp.broadcast_to(column, (KC, 128)).astype(i16)
        for j in range(EXT // 128):
            place = (lax.broadcasted_iota(i32, (KC, 128), 1) + j * 128).astype(i16)
            G[pl.ds(pl.multiple_of(s * KC, KC), KC), j * 128 : (j + 1) * 128] = jnp.where(
                wanted == place, bf16(1), bf16(0)
            )
        return carry

    lax.fori_loop(0, CELLS, build_g, 0)

    def build_s(j, carry):
        place = (lax.broadcasted_iota(i32, (256, 128), 0) + j * 256).astype(i16)
        for t in range(CELLS * KC // 128):
            wanted = jnp.broadcast_to(CR[0:1, t * 128 : (t + 1) * 128], (256, 128)).astype(i16)
            S[pl.ds(pl.multiple_of(j * 256, 256), 256), t * 128 : (t + 1) * 128] = jnp.where(
                wanted == place, bf16(1), bf16(0)
            )
        return carry

    lax.fori_loop(0, EXT // 256, build_s, 0)

    SX[0:INNER] = states[FACE : OWN - FACE]
    SX[LOW + FACE : HIGH] = states[0:FACE]
    SX[HIGH : HIGH + FACE] = states[OWN - FACE : OWN]

    @pl.when(has_low)
    def _():
        halo_up.wait_recv()

    @pl.when(jnp.logical_not(has_low))
    def _():
        SX[LOW : LOW + FACE] = jnp.zeros((FACE, COLS), f32)

    @pl.when(has_high)
    def _():
        halo_down.wait_recv()

    @pl.when(jnp.logical_not(has_high))
    def _():
        SX[HIGH + FACE : EXT] = jnp.zeros((FACE, COLS), f32)

    def set_field(at, count, value):
        hi, lo = split(value)
        E[at : at + count, 0:COLS] = hi
        E[at : at + count, COLS : 2 * COLS] = lo

    set_field(0, EXT, SX[...])

    half_rows = CELLS * KC // 2

    def gather(start, stop, first):
        def body(m, carry):
            r = pl.ds(pl.multiple_of(m * half_rows, half_rows), half_rows)
            got = jnp.dot(G[r, start:stop], E[start:stop], preferred_element_type=f32)
            if not first:
                got = got + X[r, :].astype(f32)
            X[r, :] = got.astype(bf16)
            return carry

        lax.fori_loop(0, 2, body, 0)

    gather(0, EXT, True)

    def forward(k):
        piece_copy(zpeer, k, zpeer, z_send.at[k]).wait_recv()
        for j, p in enumerate(xpeers):
            piece_copy(zpeer, k, p, f_send.at[k, j]).start()

    def put(s, at, count, lane, value):
        hi, lo = split(value)
        base, step = (at, 256) if at < 256 else (512 + at - 256, 96)
        Hs[s, base : base + count, lane : lane + 128] = hi
        Hs[s, base + step : base + step + count, lane : lane + 128] = lo

    def padded(value, count):
        return jnp.concatenate([value, jnp.zeros((count - value.shape[0], 128), f32)], axis=0)

    def unpack_b(s, e):
        for i in range(2):
            part = RX[e, PB + 88 * i : PB + 88 * (i + 1)]
            if i == 0:
                part = jnp.where(row88 == 87, 0.0, part)
            put(s, 256, 96, 128 * i, padded(part, 96))
            put(s, 128 * i, 128, 256, jnp.transpose(padded(part, 128)))

    def unpack_a(s, e):
        part = RX[e, PA : PA + 128]
        put(s, 128, 128, 0, part)
        put(s, 0, 128, 128, jnp.transpose(part))

    def unpack_d(s, e):
        part = RX[e, PD : PD + 128]
        flipped = jnp.transpose(part)
        middle = RX[e, PB + 87 : PB + 88]
        put(s, 0, 128, 0, jnp.where(row >= col, part, flipped))
        put(s, 128, 128, 128, jnp.where(row < col, part, jnp.where(row > col, flipped, middle)))

    def unpack_c(s, e):
        put(s, 256, 96, 256, padded(RX[e, PC : PC + 88], 96))

    def product(s, base, count, at):
        r = pl.ds(pl.multiple_of(s * KC, KC), KC)
        t = jnp.dot(Hs[s, base : base + 2 * count, :KC], X[r, :], preferred_element_type=f32)
        p = (t[count:, COLS:] + t[count:, :COLS]) + (t[:count, COLS:] + t[:count, :COLS])
        hi, lo = split(p)
        w = pl.ds(at, count)
        PR[w, 0:COLS] = hi
        PR[w, COLS : 2 * COLS] = lo

    def top_rows(s, at):
        product(s, 0, 256, at)

    def bottom_rows(s, at):
        product(s, 512, 96, at)

    TOPS = nx * KC
    BOTTOMS = TOPS + nx * 256

    def near_products(j):
        top_rows(j, pl.multiple_of(j * KC, 32))
        bottom_rows(j, pl.multiple_of(j * KC + 256, 32))

    def far_tops(j):
        top_rows(nx + j, pl.multiple_of(TOPS + j * 256, 128))

    def far_bottoms(j):
        bottom_rows(nx + j, pl.multiple_of(BOTTOMS + j * 96, 32))

    def scatter(at, count, start, stop, first):
        got = jnp.dot(S[at : at + count, start:stop], PR[start:stop], preferred_element_type=f32)
        got = got[:, :COLS] + got[:, COLS:]
        T[at : at + count] = got if first else T[at : at + count] + got

    def near_cell(j, carry):
        e = cell_of(j)

        @pl.when(j > 0)
        def _():
            whole_copy(e, zpeer, x_send.at[0]).wait_recv()

        unpack_b(j, e)
        unpack_a(j, e)
        unpack_d(j, e)
        unpack_c(j, e)
        near_products(j)
        return carry

    forward(0)
    lax.fori_loop(0, 2, near_cell, 0)
    forward(1)
    lax.fori_loop(2, nx, near_cell, 0)
    for at in range(0, EXT, EXT // 2):
        scatter(at, EXT // 2, 0, TOPS, True)

    def far(k, unpack):
        def body(j, carry):
            e = cell_of(nx + j)

            @pl.when(j > 0)
            def _():
                piece_copy(e, k, zpeer, z_send.at[k]).wait_recv()

            unpack(nx + j, e)
            return carry

        lax.fori_loop(0, nx, body, 0)

    far(0, unpack_b)
    far(1, unpack_a)
    forward(2)
    forward(3)
    far(2, unpack_d)

    def all_far(rows_of):
        def body(j, carry):
            rows_of(j)
            return carry

        lax.fori_loop(0, nx, body, 0)

    all_far(far_tops)
    for at in range(0, EXT, EXT // 2):
        scatter(at, EXT // 2, TOPS, BOTTOMS, False)
    far(3, unpack_c)
    all_far(far_bottoms)
    end = BOTTOMS + nx * 96
    scatter(LOW, 2 * FACE, BOTTOMS, end, False)

    @pl.when(has_low)
    def _():
        sum_down.start()

    scatter(HIGH, 2 * FACE, BOTTOMS, end, False)

    @pl.when(has_high)
    def _():
        sum_up.start()

    scatter(0, INNER, BOTTOMS, end, False)

    def set_first(at, count, total, keep=None):
        value = (total - center * SX[at : at + count]) * (1.0 / half)
        if keep is not None:
            value = jnp.where(keep, value, 0.0)
        F[at : at + count] = value
        set_field(at, count, value)

    set_first(0, INNER, T[0:INNER])
    gather(0, EARLY, True)

    @pl.when(has_low)
    def _():
        sum_up.wait_recv()

    @pl.when(jnp.logical_not(has_low))
    def _():
        XR[0] = jnp.zeros((2 * FACE, COLS), f32)

    @pl.when(has_high)
    def _():
        sum_down.wait_recv()

    @pl.when(jnp.logical_not(has_high))
    def _():
        XR[1] = jnp.zeros((2 * FACE, COLS), f32)

    set_first(LOW, FACE, T[LOW : LOW + FACE] + XR[0, 0:FACE], has_low)
    set_first(LOW + FACE, FACE, T[LOW + FACE : HIGH] + XR[0, FACE:])
    set_first(HIGH, FACE, T[HIGH : HIGH + FACE] + XR[1, 0:FACE])
    set_first(HIGH + FACE, FACE, T[HIGH + FACE : EXT] + XR[1, FACE:], has_high)
    gather(EARLY, EXT, False)

    def second_near(j, carry):
        near_products(j)
        return carry

    lax.fori_loop(0, nx, second_near, 0)

    def second_far(j, carry):
        far_tops(j)
        far_bottoms(j)
        return carry

    lax.fori_loop(0, nx, second_far, 0)

    @pl.when(has_low)
    def _():
        sum_down.wait_send()

    @pl.when(has_high)
    def _():
        sum_up.wait_send()

    scatter(LOW, FACE, 0, end, True)

    @pl.when(has_low)
    def _():
        own_down.start()

    scatter(HIGH + FACE, FACE, 0, end, True)

    @pl.when(has_high)
    def _():
        own_up.start()

    def finish(to, at, count, total):
        value = (total - center * F[at : at + count]) * (2.0 / half)
        out[to : to + count] = value - SX[at : at + count]

    scatter(0, INNER, 0, end, True)
    finish(FACE, 0, INNER, T[0:INNER])
    scatter(LOW + FACE, 2 * FACE, 0, end, True)

    @pl.when(has_low)
    def _():
        own_up.wait_recv()

    @pl.when(jnp.logical_not(has_low))
    def _():
        YR[0] = jnp.zeros((FACE, COLS), f32)

    @pl.when(has_high)
    def _():
        own_down.wait_recv()

    @pl.when(jnp.logical_not(has_high))
    def _():
        YR[1] = jnp.zeros((FACE, COLS), f32)

    finish(0, LOW + FACE, FACE, T[LOW + FACE : HIGH] + YR[0])
    finish(OWN - FACE, HIGH, FACE, T[HIGH : HIGH + FACE] + YR[1])

    for c in z_copies + x_copies:
        c.wait_send()
    for k in range(4):
        for j, p in enumerate(xpeers):
            piece_copy(zpeer, k, p, f_send.at[k, j]).wait_send()

    @pl.when(has_low)
    def _():
        halo_down.wait_send()
        own_down.wait_send()

    @pl.when(has_high)
    def _():
        halo_up.wait_send()
        own_up.wait_send()


def on_device(states, connectivity, cell_hamiltonian):
    vmem = pl.BlockSpec(memory_space=pltpu.VMEM)
    kt = CELLS * KC
    return pl.pallas_call(
        kernel,
        out_shape=jax.ShapeDtypeStruct((OWN, COLS), f32),
        in_specs=[vmem] * 3,
        out_specs=vmem,
        scratch_shapes=[
            pltpu.VMEM((kt, EXT), bf16),
            pltpu.VMEM((EXT, kt), bf16),
            pltpu.VMEM((CELLS, 2 * KC, 384), bf16),
            pltpu.VMEM((kt, 2 * COLS), bf16),
            pltpu.VMEM((kt, 2 * COLS), bf16),
            pltpu.VMEM((EXT, 2 * COLS), bf16),
            pltpu.VMEM((CELLS, PROWS, 128), f32),
            pltpu.VMEM((EXT, COLS), f32),
            pltpu.VMEM((EXT, COLS), f32),
            pltpu.VMEM((EXT, COLS), f32),
            pltpu.VMEM((2, 2 * FACE, COLS), f32),
            pltpu.VMEM((2, FACE, COLS), f32),
            pltpu.VMEM((KC, 384), f32),
            pltpu.VMEM((CELLS, 384), i32),
            pltpu.VMEM((1, kt), i32),
            pltpu.SemaphoreType.DMA((4,)),
            pltpu.SemaphoreType.DMA((3,)),
            pltpu.SemaphoreType.DMA((4, 3)),
            pltpu.SemaphoreType.DMA((6,)),
            pltpu.SemaphoreType.DMA((CELLS, 4)),
            pltpu.SemaphoreType.DMA((6,)),
        ],
        compiler_params=pltpu.CompilerParams(
            collective_id=0, has_side_effects=True, vmem_limit_bytes=58 << 20
        ),
    )(states, connectivity, cell_hamiltonian)


def solution(mesh):
    return jax.shard_map(
        on_device,
        mesh=mesh,
        in_specs=(P("domain", "band"), P("domain", None), P(("domain", "band"), None, None)),
        out_specs=P("domain", "band"),
        check_vma=False,
    )
```

```python
import functools

import jax
import jax.numpy as jnp
from jax import lax
from jax.experimental import pallas as pl
from jax.experimental.pallas import tpu as pltpu
from jax.sharding import PartitionSpec as P

MESH = pl.DeviceIdType.MESH
f32, bf16, i32, i16 = jnp.float32, jnp.bfloat16, jnp.int32, jnp.int16

NPC = 343
KC = 352
CELLS = 8
FACE = 288
OWN = 1728
EXT = OWN + 2 * FACE
COLS = 128
INNER = OWN - 2 * FACE

LOW = INNER
HIGH = INNER + 2 * FACE
EARLY = 1024

PB, PA, PD, PC, PROWS = 0, 176, 304, 432, 480
PIECES = ((PB, 176), (PA, 128), (PD, 128), (PC, 48))

center = 0.5
half = 1.5


def split(value):
    hi = value.astype(bf16)
    lo = (value - hi.astype(f32)).astype(bf16)
    return hi, lo


def rows_cols(rows):
    return lax.broadcasted_iota(i32, (rows, 128), 0), lax.broadcasted_iota(i32, (rows, 128), 1)


def padded(value, count):
    return jnp.concatenate([value, jnp.zeros((count - value.shape[0], 128), f32)], axis=0)


def pack_corner(corner, roll):
    row, col = rows_cols(48)
    second = padded(roll(corner[48:88], 80), 48)
    both = jnp.where(row >= col, corner[0:48], second)
    diag = jnp.sum(jnp.where(row == col, second, 0.0), axis=1, keepdims=True)
    below = padded(corner[48:88], 48)
    packed = jnp.where(col < 48, below, jnp.where((col >= 64) & (col < 112), roll(both, 64), 0.0))
    return jnp.where(col == 127, diag, packed)


def unpack_corner(packed, roll):
    row, col = rows_cols(48)
    flipped = jnp.transpose(padded(packed, 128))
    both = roll(packed, 64)
    both_t = flipped[64:112]
    first = jnp.where(row >= col, both, both_t)
    second = jnp.where(row < col, both, jnp.where(row > col, both_t, packed[:, 127:128]))
    upper = jnp.where(col < 48, first, jnp.where(col < 88, roll(flipped[0:48], 48), 0.0))
    lower = jnp.where(col < 48, packed, jnp.where(col < 88, roll(second, 48), 0.0))
    return jnp.concatenate([upper, lower[0:40]], axis=0)


def lane_roll(value, shift):
    return pltpu.roll(value, shift, 1)


def kernel(
    states, conn, cell, out,
    G, S, Hs, X, PR, E, RX, T, SX, F, XR, YR, Hf, CP, CR, CN, V, O,
    z_send, x_send, f_send, n_send, cell_recv, n_recv, local,
):
    d = lax.axis_index("domain")
    b = lax.axis_index("band")
    last = lax.axis_size("domain") - 1
    nx = CELLS // 2
    xi = b // 2
    zh = b % 2
    zpeer = 2 * xi + 1 - zh
    xpeers = [2 * ((xi + j) % nx) + zh for j in (1, 3, 2)]
    has_low = d > 0
    has_high = d < last

    barrier = pltpu.get_barrier_semaphore()

    def greet(dd, bb):
        pl.semaphore_signal(barrier, inc=1, device_id=(dd, bb), device_id_type=MESH)

    greet(d, zpeer)
    for p in xpeers:
        greet(d, p)

    @pl.when(has_low)
    def _():
        greet(d - 1, b)

    @pl.when(has_high)
    def _():
        greet(d + 1, b)

    load_cell = pltpu.make_async_copy(cell, V, local.at[0])
    load_conn = pltpu.make_async_copy(conn, CN, local.at[1])
    loads = [
        pltpu.make_async_copy(states.at[pl.ds(a, c)], SX.at[pl.ds(to, c)], local.at[2 + i])
        for i, (a, c, to) in enumerate(
            ((0, FACE, LOW + FACE), (OWN - FACE, FACE, HIGH), (FACE, INNER, 0))
        )
    ]
    for c in [load_cell, load_conn] + loads:
        c.start()

    Hf[...] = jnp.zeros_like(Hf)
    load_cell.wait()
    Hf[0:NPC, 0:NPC] = V[:, 0, :]
    row, col = rows_cols(128)
    row88 = rows_cols(88)[0]
    d2 = Hf[128:256, 128:256]
    diag = jnp.sum(jnp.where(row == col, d2, 0.0), axis=0, keepdims=True)
    RX[b, PB : PB + 88] = jnp.where(row88 == 87, diag, Hf[256:344, 0:128])
    RX[b, PB + 88 : PB + 176] = Hf[256:344, 128:256]
    RX[b, PA : PA + 128] = Hf[128:256, 0:128]
    RX[b, PD : PD + 128] = jnp.where(row >= col, Hf[0:128, 0:128], d2)
    RX[b, PC : PC + 48] = pack_corner(Hf[256:344, 256:384], lane_roll)

    pl.semaphore_wait(barrier, 4 + has_low.astype(i32) + has_high.astype(i32))

    def piece_copy(e, k, target, send_sem):
        at, rows = PIECES[k]
        part = RX.at[e, pl.ds(at, rows)]
        return pltpu.make_async_remote_copy(
            src_ref=part, dst_ref=part, send_sem=send_sem, recv_sem=cell_recv.at[e, k],
            device_id=(d, target), device_id_type=MESH,
        )

    def whole_copy(e, target, send_sem):
        return pltpu.make_async_remote_copy(
            src_ref=RX.at[e], dst_ref=RX.at[e], send_sem=send_sem, recv_sem=cell_recv.at[e, 0],
            device_id=(d, target), device_id_type=MESH,
        )

    def node_copy(src, dst, i, dd):
        return pltpu.make_async_remote_copy(
            src_ref=src, dst_ref=dst, send_sem=n_send.at[i], recv_sem=n_recv.at[i],
            device_id=(dd, b), device_id_type=MESH,
        )

    z_copies = [piece_copy(b, k, zpeer, z_send.at[k]) for k in range(4)]
    for c in z_copies:
        c.start()
    x_copies = [whole_copy(b, p, x_send.at[j]) for j, p in enumerate(xpeers)]
    for c in x_copies:
        c.start()

    def exchange(step, down_src, down_dst, up_src, up_dst):
        down = node_copy(down_src, down_dst, 2 * step, d - 1)
        up = node_copy(up_src, up_dst, 2 * step + 1, d + 1)
        return down, up

    halo_down, halo_up = exchange(
        0, SX.at[pl.ds(LOW + FACE, FACE)], SX.at[pl.ds(HIGH + FACE, FACE)],
        SX.at[pl.ds(HIGH, FACE)], SX.at[pl.ds(LOW, FACE)],
    )
    sum_down, sum_up = exchange(
        1, T.at[pl.ds(LOW, 2 * FACE)], XR.at[1], T.at[pl.ds(HIGH, 2 * FACE)], XR.at[0]
    )
    own_down, own_up = exchange(
        2, T.at[pl.ds(LOW, FACE)], YR.at[1], T.at[pl.ds(HIGH + FACE, FACE)], YR.at[0]
    )

    loads[0].wait()
    loads[1].wait()

    @pl.when(has_low)
    def _():
        halo_down.start()

    @pl.when(has_high)
    def _():
        halo_up.start()

    CP[...] = jnp.full(CP.shape, -1, i32)
    load_conn.wait()
    n = CN[...]
    CP[:, 0:NPC] = jnp.where(n < 2 * FACE, n + LOW, jnp.where(n < OWN, n - 2 * FACE, n))

    def cell_of(s):
        side = s // nx
        return 2 * ((xi + s) % nx) + zh + side * (1 - 2 * zh)

    rows = [CP[pl.ds(cell_of(s), 1), :] for s in range(CELLS)]
    near = [r[:, :KC] for r in rows[:nx]]
    top = [r[:, :256] for r in rows[nx:]]
    bottom = [r[:, 256:KC] for r in rows[nx:]]
    CR[...] = jnp.concatenate(near + top + bottom, axis=1)

    def build_g(s, carry):
        line = jnp.broadcast_to(CP[pl.ds(cell_of(s), 1), :], (8, 384))
        column = jnp.transpose(line)[:KC, 0:1]
        wanted = jnp.broadcast_to(column, (KC, 128)).astype(i16)
        for j in range(EXT // 128):
            place = (lax.broadcasted_iota(i32, (KC, 128), 1) + j * 128).astype(i16)
            G[pl.ds(pl.multiple_of(s * KC, KC), KC), j * 128 : (j + 1) * 128] = jnp.where(
                wanted == place, bf16(1), bf16(0)
            )
        return carry

    lax.fori_loop(0, CELLS, build_g, 0)

    def build_s(j, carry):
        place = (lax.broadcasted_iota(i32, (256, 128), 0) + j * 256).astype(i16)
        for t in range(CELLS * KC // 128):
            wanted = jnp.broadcast_to(CR[0:1, t * 128 : (t + 1) * 128], (256, 128)).astype(i16)
            S[pl.ds(pl.multiple_of(j * 256, 256), 256), t * 128 : (t + 1) * 128] = jnp.where(
                wanted == place, bf16(1), bf16(0)
            )
        return carry

    lax.fori_loop(0, EXT // 256, build_s, 0)

    loads[2].wait()

    @pl.when(has_low)
    def _():
        halo_up.wait_recv()

    @pl.when(jnp.logical_not(has_low))
    def _():
        SX[LOW : LOW + FACE] = jnp.zeros((FACE, COLS), f32)

    @pl.when(has_high)
    def _():
        halo_down.wait_recv()

    @pl.when(jnp.logical_not(has_high))
    def _():
        SX[HIGH + FACE : EXT] = jnp.zeros((FACE, COLS), f32)

    def set_field(at, count, value):
        hi, lo = split(value)
        E[at : at + count, 0:COLS] = hi
        E[at : at + count, COLS : 2 * COLS] = lo

    set_field(0, EXT, SX[...])

    half_rows = CELLS * KC // 2

    def gather(start, stop, first):
        def body(m, carry):
            r = pl.ds(pl.multiple_of(m * half_rows, half_rows), half_rows)
            got = jnp.dot(G[r, start:stop], E[start:stop], preferred_element_type=f32)
            if not first:
                got = got + X[r, :].astype(f32)
            X[r, :] = got.astype(bf16)
            return carry

        lax.fori_loop(0, 2, body, 0)

    gather(0, EXT, True)

    def forward(k):
        piece_copy(zpeer, k, zpeer, z_send.at[k]).wait_recv()
        for j, p in enumerate(xpeers):
            piece_copy(zpeer, k, p, f_send.at[k, j]).start()

    def put(s, at, count, lane, value):
        hi, lo = split(value)
        base, step = (at, 256) if at < 256 else (512 + at - 256, 96)
        Hs[s, base : base + count, lane : lane + 128] = hi
        Hs[s, base + step : base + step + count, lane : lane + 128] = lo

    def unpack_b(s, e):
        for i in range(2):
            part = RX[e, PB + 88 * i : PB + 88 * (i + 1)]
            if i == 0:
                part = jnp.where(row88 == 87, 0.0, part)
            put(s, 256, 96, 128 * i, padded(part, 96))
            put(s, 128 * i, 128, 256, jnp.transpose(padded(part, 128)))

    def unpack_a(s, e):
        part = RX[e, PA : PA + 128]
        put(s, 128, 128, 0, part)
        put(s, 0, 128, 128, jnp.transpose(part))

    def unpack_d(s, e):
        part = RX[e, PD : PD + 128]
        flipped = jnp.transpose(part)
        middle = RX[e, PB + 87 : PB + 88]
        put(s, 0, 128, 0, jnp.where(row >= col, part, flipped))
        put(s, 128, 128, 128, jnp.where(row < col, part, jnp.where(row > col, flipped, middle)))

    def unpack_c(s, e):
        put(s, 256, 96, 256, padded(unpack_corner(RX[e, PC : PC + 48], lane_roll), 96))

    TOPS = nx * KC
    BOTTOMS = TOPS + nx * 256

    def product(s, base, count, *parts):
        t = jnp.dot(
            Hs[s, base : base + count, :KC], X[s * KC : (s + 1) * KC], preferred_element_type=f32
        )
        for at, rows, to in parts:
            hi_part, lo_part = t[at : at + rows], t[at + rows : at + 2 * rows]
            p = (lo_part[:, COLS:] + lo_part[:, :COLS]) + (hi_part[:, COLS:] + hi_part[:, :COLS])
            hi, lo = split(p)
            PR[to : to + rows, 0:COLS] = hi
            PR[to : to + rows, COLS : 2 * COLS] = lo

    def near_products():
        for j in range(nx):
            product(j, 0, 704, (0, 256, j * KC), (512, 96, j * KC + 256))

    def far_tops():
        for j in range(nx):
            product(nx + j, 0, 512, (0, 256, TOPS + j * 256))

    def far_bottoms():
        for j in range(nx):
            product(nx + j, 512, 192, (0, 96, BOTTOMS + j * 96))

    def far_products():
        for j in range(nx):
            product(nx + j, 0, 704, (0, 256, TOPS + j * 256), (512, 96, BOTTOMS + j * 96))

    def scatter(at, count, start, stop, first):
        got = jnp.dot(S[at : at + count, start:stop], PR[start:stop], preferred_element_type=f32)
        got = got[:, :COLS] + got[:, COLS:]
        T[at : at + count] = got if first else T[at : at + count] + got

    def near_cell(j, carry):
        e = cell_of(j)

        @pl.when(j > 0)
        def _():
            whole_copy(e, zpeer, x_send.at[0]).wait_recv()

        unpack_b(j, e)
        unpack_a(j, e)
        unpack_d(j, e)
        unpack_c(j, e)
        return carry

    def far(k, unpack):
        cells = [cell_of(nx + j) for j in range(nx)]
        for e in cells[1:]:
            piece_copy(e, k, zpeer, z_send.at[k]).wait_recv()
        for j, e in enumerate(cells):
            unpack(nx + j, e)

    forward(0)
    lax.fori_loop(0, nx, near_cell, 0)
    near_products()
    for at in range(0, EXT, EXT // 2):
        scatter(at, EXT // 2, 0, TOPS, True)
    forward(1)
    far(0, unpack_b)
    forward(2)
    far(1, unpack_a)
    forward(3)
    far(2, unpack_d)
    far_tops()
    for at in range(0, EXT, EXT // 2):
        scatter(at, EXT // 2, TOPS, BOTTOMS, False)
    far(3, unpack_c)
    far_bottoms()
    end = BOTTOMS + nx * 96
    scatter(LOW, 2 * FACE, BOTTOMS, end, False)

    @pl.when(has_low)
    def _():
        sum_down.start()

    scatter(HIGH, 2 * FACE, BOTTOMS, end, False)

    @pl.when(has_high)
    def _():
        sum_up.start()

    scatter(0, INNER, BOTTOMS, end, False)

    def set_first(at, count, total, keep=None):
        value = (total - center * SX[at : at + count]) * (1.0 / half)
        if keep is not None:
            value = jnp.where(keep, value, 0.0)
        F[at : at + count] = value
        set_field(at, count, value)

    set_first(0, INNER, T[0:INNER])
    gather(0, EARLY, True)

    @pl.when(has_low)
    def _():
        sum_up.wait_recv()

    @pl.when(jnp.logical_not(has_low))
    def _():
        XR[0] = jnp.zeros((2 * FACE, COLS), f32)

    @pl.when(has_high)
    def _():
        sum_down.wait_recv()

    @pl.when(jnp.logical_not(has_high))
    def _():
        XR[1] = jnp.zeros((2 * FACE, COLS), f32)

    set_first(LOW, FACE, T[LOW : LOW + FACE] + XR[0, 0:FACE], has_low)
    set_first(LOW + FACE, FACE, T[LOW + FACE : HIGH] + XR[0, FACE:])
    set_first(HIGH, FACE, T[HIGH : HIGH + FACE] + XR[1, 0:FACE])
    set_first(HIGH + FACE, FACE, T[HIGH + FACE : EXT] + XR[1, FACE:], has_high)
    gather(EARLY, EXT, False)

    near_products()
    far_products()

    @pl.when(has_low)
    def _():
        sum_down.wait_send()

    @pl.when(has_high)
    def _():
        sum_up.wait_send()

    scatter(LOW, FACE, 0, end, True)

    @pl.when(has_low)
    def _():
        own_down.start()

    scatter(HIGH + FACE, FACE, 0, end, True)

    @pl.when(has_high)
    def _():
        own_up.start()

    def finish(i, to, at, count, total):
        O[to : to + count] = (total - center * F[at : at + count]) * (2.0 / half)
        part = pl.ds(to, count)
        store = pltpu.make_async_copy(O.at[part], out.at[part], local.at[i])
        store.start()
        return store

    scatter(0, INNER, 0, end, True)
    stores = [finish(0, FACE, 0, INNER, T[0:INNER])]
    scatter(LOW + FACE, 2 * FACE, 0, end, True)

    @pl.when(has_low)
    def _():
        own_up.wait_recv()

    @pl.when(jnp.logical_not(has_low))
    def _():
        YR[0] = jnp.zeros((FACE, COLS), f32)

    @pl.when(has_high)
    def _():
        own_down.wait_recv()

    @pl.when(jnp.logical_not(has_high))
    def _():
        YR[1] = jnp.zeros((FACE, COLS), f32)

    stores.append(finish(1, 0, LOW + FACE, FACE, T[LOW + FACE : HIGH] + YR[0]))
    stores.append(finish(2, OWN - FACE, HIGH, FACE, T[HIGH : HIGH + FACE] + YR[1]))

    for c in z_copies + x_copies:
        c.wait_send()
    for k in range(4):
        for j, p in enumerate(xpeers):
            piece_copy(zpeer, k, p, f_send.at[k, j]).wait_send()

    @pl.when(has_low)
    def _():
        halo_down.wait_send()
        own_down.wait_send()

    @pl.when(has_high)
    def _():
        halo_up.wait_send()
        own_up.wait_send()

    for c in stores:
        c.wait()


def on_device(states, connectivity, cell_hamiltonian):
    anywhere = pl.BlockSpec(memory_space=pl.ANY)
    kt = CELLS * KC
    moved = pl.pallas_call(
        kernel,
        out_shape=jax.ShapeDtypeStruct((OWN, COLS), f32),
        in_specs=[anywhere] * 3,
        out_specs=anywhere,
        scratch_shapes=[
            pltpu.VMEM((kt, EXT), bf16),
            pltpu.VMEM((EXT, kt), bf16),
            pltpu.VMEM((CELLS, 2 * KC, 384), bf16),
            pltpu.VMEM((kt, 2 * COLS), bf16),
            pltpu.VMEM((kt, 2 * COLS), bf16),
            pltpu.VMEM((EXT, 2 * COLS), bf16),
            pltpu.VMEM((CELLS, PROWS, 128), f32),
            pltpu.VMEM((EXT, COLS), f32),
            pltpu.VMEM((EXT, COLS), f32),
            pltpu.VMEM((EXT, COLS), f32),
            pltpu.VMEM((2, 2 * FACE, COLS), f32),
            pltpu.VMEM((2, FACE, COLS), f32),
            pltpu.VMEM((KC, 384), f32),
            pltpu.VMEM((CELLS, 384), i32),
            pltpu.VMEM((1, kt), i32),
            pltpu.VMEM((CELLS, NPC), i32),
            pltpu.VMEM((NPC, 1, NPC), f32),
            pltpu.VMEM((OWN, COLS), f32),
            pltpu.SemaphoreType.DMA((4,)),
            pltpu.SemaphoreType.DMA((3,)),
            pltpu.SemaphoreType.DMA((4, 3)),
            pltpu.SemaphoreType.DMA((6,)),
            pltpu.SemaphoreType.DMA((CELLS, 4)),
            pltpu.SemaphoreType.DMA((6,)),
            pltpu.SemaphoreType.DMA((5,)),
        ],
        compiler_params=pltpu.CompilerParams(
            collective_id=0, has_side_effects=True, vmem_limit_bytes=58 << 20
        ),
    )(states, connectivity, cell_hamiltonian.reshape(NPC, 1, NPC))
    return moved - states


def solution(mesh):
    return jax.shard_map(
        on_device,
        mesh=mesh,
        in_specs=(P("domain", "band"), P("domain", None), P(("domain", "band"), None, None)),
        out_specs=P("domain", "band"),
        check_vma=False,
    )
```

```python
import functools

import jax
import jax.numpy as jnp
from jax import lax
from jax.experimental import pallas as pl
from jax.experimental.pallas import tpu as pltpu
from jax.sharding import PartitionSpec as P

MESH = pl.DeviceIdType.MESH
f32, bf16, i32, i16 = jnp.float32, jnp.bfloat16, jnp.int32, jnp.int16

NPC = 343
KC = 352
CELLS = 8
FACE = 288
OWN = 1728
EXT = OWN + 2 * FACE
COLS = 128
INNER = OWN - 2 * FACE

LOW = INNER
HIGH = INNER + 2 * FACE
EARLY = 1024

PB, PA, PC, PD, PROWS = 0, 176, 304, 352, 480
PIECES = ((0, 88), (88, 88), (176, 88), (264, 88), (352, 64), (416, 64))
HOP = 4

center = 0.5
half = 1.5


def split(value):
    hi = value.astype(bf16)
    lo = (value - hi.astype(f32)).astype(bf16)
    return hi, lo


def rows_cols(rows):
    return lax.broadcasted_iota(i32, (rows, 128), 0), lax.broadcasted_iota(i32, (rows, 128), 1)


def padded(value, count):
    return jnp.concatenate([value, jnp.zeros((count - value.shape[0], 128), f32)], axis=0)


def pack_corner(corner, roll):
    row, col = rows_cols(48)
    second = padded(roll(corner[48:88], 80), 48)
    both = jnp.where(row >= col, corner[0:48], second)
    diag = jnp.sum(jnp.where(row == col, second, 0.0), axis=1, keepdims=True)
    below = padded(corner[48:88], 48)
    packed = jnp.where(col < 48, below, jnp.where((col >= 64) & (col < 112), roll(both, 64), 0.0))
    return jnp.where(col == 127, diag, packed)


def unpack_corner(packed, roll):
    row, col = rows_cols(48)
    flipped = jnp.transpose(padded(packed, 128))
    both = roll(packed, 64)
    both_t = flipped[64:112]
    first = jnp.where(row >= col, both, both_t)
    second = jnp.where(row < col, both, jnp.where(row > col, both_t, packed[:, 127:128]))
    upper = jnp.where(col < 48, first, jnp.where(col < 88, roll(flipped[0:48], 48), 0.0))
    lower = jnp.where(col < 48, packed, jnp.where(col < 88, roll(second, 48), 0.0))
    return jnp.concatenate([upper, lower[0:40]], axis=0)


def lane_roll(value, shift):
    return pltpu.roll(value, shift, 1)


def kernel(
    states, conn, cell, out,
    G, S, Hs, X, PR, E, RX, T, SX, F, XR, YR, Hf, CP, CR, CN, V, O,
    RL, z_send, z_recv, x_send, f_send, n_send, cell_recv, n_recv, local,
):
    d = lax.axis_index("domain")
    b = lax.axis_index("band")
    last = lax.axis_size("domain") - 1
    nx = CELLS // 2
    xi = b // 2
    zh = b % 2
    zpeer = 2 * xi + 1 - zh
    xpeers = [2 * ((xi + j) % nx) + zh for j in (1, 3, 2)]
    z = 8 * zh + d // 8

    def along_z(way):
        to = (z + (HOP, 16 - HOP)[way]) % 16
        return (to % 8) * 8 + d % 8, 2 * xi + to // 8, to // 8

    has_low = d > 0
    has_high = d < last

    barrier = pltpu.get_barrier_semaphore()

    def greet(dd, bb):
        pl.semaphore_signal(barrier, inc=1, device_id=(dd, bb), device_id_type=MESH)

    for way in range(2):
        greet(*along_z(way)[:2])
    for p in xpeers:
        greet(d, p)

    @pl.when(has_low)
    def _():
        greet(d - 1, b)

    @pl.when(has_high)
    def _():
        greet(d + 1, b)

    load_cell = pltpu.make_async_copy(cell, V, local.at[0])
    load_conn = pltpu.make_async_copy(conn, CN, local.at[1])
    loads = [
        pltpu.make_async_copy(states.at[pl.ds(a, c)], SX.at[pl.ds(to, c)], local.at[2 + i])
        for i, (a, c, to) in enumerate(
            ((0, FACE, LOW + FACE), (OWN - FACE, FACE, HIGH), (FACE, INNER, 0))
        )
    ]
    for c in [load_cell, load_conn] + loads:
        c.start()

    Hf[...] = jnp.zeros_like(Hf)
    load_cell.wait()
    Hf[0:NPC, 0:NPC] = V[:, 0, :]
    row, col = rows_cols(128)
    row88 = rows_cols(88)[0]
    d2 = Hf[128:256, 128:256]
    diag = jnp.sum(jnp.where(row == col, d2, 0.0), axis=0, keepdims=True)
    RX[b, PB : PB + 88] = jnp.where(row88 == 87, diag, Hf[256:344, 0:128])
    RX[b, PB + 88 : PB + 176] = Hf[256:344, 128:256]
    RX[b, PA : PA + 128] = Hf[128:256, 0:128]
    RX[b, PD : PD + 128] = jnp.where(row >= col, Hf[0:128, 0:128], d2)
    RX[b, PC : PC + 48] = pack_corner(Hf[256:344, 256:384], lane_roll)

    pl.semaphore_wait(barrier, 5 + has_low.astype(i32) + has_high.astype(i32))

    def piece_copy(e, k, target, send_sem):
        part = RX.at[e, pl.ds(*PIECES[k])]
        return pltpu.make_async_remote_copy(
            src_ref=part, dst_ref=part, send_sem=send_sem, recv_sem=cell_recv.at[e, k],
            device_id=(d, target), device_id_type=MESH,
        )

    def whole_copy(e, target, send_sem):
        return pltpu.make_async_remote_copy(
            src_ref=RX.at[e], dst_ref=RX.at[e], send_sem=send_sem, recv_sem=cell_recv.at[e, 0],
            device_id=(d, target), device_id_type=MESH,
        )

    def node_copy(src, dst, i, dd):
        return pltpu.make_async_remote_copy(
            src_ref=src, dst_ref=dst, send_sem=n_send.at[i], recv_sem=n_recv.at[i],
            device_id=(dd, b), device_id_type=MESH,
        )

    def z_copy(leg, k):
        dd, bb, side = along_z(k % 2)
        rows = pl.ds(*PIECES[k])
        return pltpu.make_async_remote_copy(
            src_ref=RL.at[rows] if leg else RX.at[b, rows],
            dst_ref=RX.at[2 * xi + 1 - side, rows] if leg else RL.at[rows],
            send_sem=z_send.at[leg, k], recv_sem=z_recv.at[leg, k],
            device_id=(dd, bb), device_id_type=MESH,
        )

    for k in range(4):
        z_copy(0, k).start()
    x_copies = [whole_copy(b, p, x_send.at[j]) for j, p in enumerate(xpeers)]
    for c in x_copies:
        c.start()

    def exchange(step, down_src, down_dst, up_src, up_dst):
        down = node_copy(down_src, down_dst, 2 * step, d - 1)
        up = node_copy(up_src, up_dst, 2 * step + 1, d + 1)
        return down, up

    halo_down, halo_up = exchange(
        0, SX.at[pl.ds(LOW + FACE, FACE)], SX.at[pl.ds(HIGH + FACE, FACE)],
        SX.at[pl.ds(HIGH, FACE)], SX.at[pl.ds(LOW, FACE)],
    )
    sum_down, sum_up = exchange(
        1, T.at[pl.ds(LOW, 2 * FACE)], XR.at[1], T.at[pl.ds(HIGH, 2 * FACE)], XR.at[0]
    )
    own_down, own_up = exchange(
        2, T.at[pl.ds(LOW, FACE)], YR.at[1], T.at[pl.ds(HIGH + FACE, FACE)], YR.at[0]
    )

    loads[0].wait()
    loads[1].wait()

    @pl.when(has_low)
    def _():
        halo_down.start()

    @pl.when(has_high)
    def _():
        halo_up.start()

    CP[...] = jnp.full(CP.shape, -1, i32)
    load_conn.wait()
    n = CN[...]
    CP[:, 0:NPC] = jnp.where(n < 2 * FACE, n + LOW, jnp.where(n < OWN, n - 2 * FACE, n))

    def cell_of(s):
        side = s // nx
        return 2 * ((xi + s) % nx) + zh + side * (1 - 2 * zh)

    rows = [CP[pl.ds(cell_of(s), 1), :] for s in range(CELLS)]
    near = [r[:, :KC] for r in rows[:nx]]
    top = [r[:, :256] for r in rows[nx:]]
    bottom = [r[:, 256:KC] for r in rows[nx:]]
    CR[...] = jnp.concatenate(near + top + bottom, axis=1)

    def build_g(s, carry):
        line = jnp.broadcast_to(CP[pl.ds(cell_of(s), 1), :], (8, 384))
        column = jnp.transpose(line)[:KC, 0:1]
        wanted = jnp.broadcast_to(column, (KC, 128)).astype(i16)
        for j in range(EXT // 128):
            place = (lax.broadcasted_iota(i32, (KC, 128), 1) + j * 128).astype(i16)
            G[pl.ds(pl.multiple_of(s * KC, KC), KC), j * 128 : (j + 1) * 128] = jnp.where(
                wanted == place, bf16(1), bf16(0)
            )
        return carry

    lax.fori_loop(0, CELLS, build_g, 0)

    def build_s(j, carry):
        place = (lax.broadcasted_iota(i32, (256, 128), 0) + j * 256).astype(i16)
        for t in range(CELLS * KC // 128):
            wanted = jnp.broadcast_to(CR[0:1, t * 128 : (t + 1) * 128], (256, 128)).astype(i16)
            S[pl.ds(pl.multiple_of(j * 256, 256), 256), t * 128 : (t + 1) * 128] = jnp.where(
                wanted == place, bf16(1), bf16(0)
            )
        return carry

    lax.fori_loop(0, EXT // 256, build_s, 0)

    loads[2].wait()

    @pl.when(has_low)
    def _():
        halo_up.wait_recv()

    @pl.when(jnp.logical_not(has_low))
    def _():
        SX[LOW : LOW + FACE] = jnp.zeros((FACE, COLS), f32)

    @pl.when(has_high)
    def _():
        halo_down.wait_recv()

    @pl.when(jnp.logical_not(has_high))
    def _():
        SX[HIGH + FACE : EXT] = jnp.zeros((FACE, COLS), f32)

    def set_field(at, count, value):
        hi, lo = split(value)
        E[at : at + count, 0:COLS] = hi
        E[at : at + count, COLS : 2 * COLS] = lo

    set_field(0, EXT, SX[...])

    half_rows = CELLS * KC // 2

    def gather_half(m, start, stop, first):
        r = pl.ds(pl.multiple_of(m * half_rows, half_rows), half_rows)
        got = jnp.dot(G[r, start:stop], E[start:stop], preferred_element_type=f32)
        if not first:
            got = got + X[r, :].astype(f32)
        X[r, :] = got.astype(bf16)

    def gather(start, stop, first):
        def body(m, carry):
            gather_half(m, start, stop, first)
            return carry

        lax.fori_loop(0, 2, body, 0)

    def relay(group):
        for k in (2 * group, 2 * group + 1):
            z_copy(0, k).wait_recv()
            z_copy(1, k).start()

    def forward(group):
        for k in (2 * group, 2 * group + 1):
            z_copy(1, k).wait_recv()
            for j, p in enumerate(xpeers):
                piece_copy(zpeer, k, p, f_send.at[k, j]).start()

    def put(s, at, count, lane, value):
        hi, lo = split(value)
        base, step = (at, 256) if at < 256 else (512 + at - 256, 96)
        Hs[s, base : base + count, lane : lane + 128] = hi
        Hs[s, base + step : base + step + count, lane : lane + 128] = lo

    def unpack_b(s, e):
        for i in range(2):
            part = RX[e, PB + 88 * i : PB + 88 * (i + 1)]
            if i == 0:
                part = jnp.where(row88 == 87, 0.0, part)
            put(s, 256, 96, 128 * i, padded(part, 96))
            put(s, 128 * i, 128, 256, jnp.transpose(padded(part, 128)))

    def unpack_a(s, e):
        part = RX[e, PA : PA + 128]
        put(s, 128, 128, 0, part)
        put(s, 0, 128, 128, jnp.transpose(part))

    def unpack_d(s, e):
        part = RX[e, PD : PD + 128]
        flipped = jnp.transpose(part)
        middle = RX[e, PB + 87 : PB + 88]
        put(s, 0, 128, 0, jnp.where(row >= col, part, flipped))
        put(s, 128, 128, 128, jnp.where(row < col, part, jnp.where(row > col, flipped, middle)))

    def unpack_c(s, e):
        put(s, 256, 96, 256, padded(unpack_corner(RX[e, PC : PC + 48], lane_roll), 96))

    TOPS = nx * KC
    BOTTOMS = TOPS + nx * 256

    def product(s, base, count, *parts):
        t = jnp.dot(
            Hs[s, base : base + count, :KC], X[s * KC : (s + 1) * KC], preferred_element_type=f32
        )
        for at, rows, to in parts:
            hi_part, lo_part = t[at : at + rows], t[at + rows : at + 2 * rows]
            p = (lo_part[:, COLS:] + lo_part[:, :COLS]) + (hi_part[:, COLS:] + hi_part[:, :COLS])
            hi, lo = split(p)
            PR[to : to + rows, 0:COLS] = hi
            PR[to : to + rows, COLS : 2 * COLS] = lo

    def near_products():
        for j in range(nx):
            product(j, 0, 704, (0, 256, j * KC), (512, 96, j * KC + 256))

    def far_tops():
        for j in range(nx):
            product(nx + j, 0, 512, (0, 256, TOPS + j * 256))

    def far_bottoms():
        for j in range(nx):
            product(nx + j, 512, 192, (0, 96, BOTTOMS + j * 96))

    def far_products():
        for j in range(nx):
            product(nx + j, 0, 704, (0, 256, TOPS + j * 256), (512, 96, BOTTOMS + j * 96))

    def scatter(at, count, start, stop, first):
        w = pl.ds(at, count)
        got = jnp.dot(S[w, start:stop], PR[start:stop], preferred_element_type=f32)
        got = got[:, :COLS] + got[:, COLS:]
        T[w, :] = got if first else T[w, :] + got

    def near_cell(j, carry):
        e = cell_of(j)

        @pl.when(j > 0)
        def _():
            whole_copy(e, zpeer, x_send.at[0]).wait_recv()

        unpack_b(j, e)
        unpack_a(j, e)
        unpack_d(j, e)
        unpack_c(j, e)
        return carry

    far_cells = [cell_of(nx + j) for j in range(nx)]

    def arrived(group):
        for e in far_cells[1:]:
            for k in (2 * group, 2 * group + 1):
                piece_copy(e, k, zpeer, z_send.at[0, k]).wait_recv()

    core = d % 2
    down_first = core == 0

    def start_both(down, up):
        def begin(place):
            @pl.when(has_low & (down_first if place == 0 else jnp.logical_not(down_first)))
            def _():
                down.start()

            @pl.when(has_high & (jnp.logical_not(down_first) if place == 0 else down_first))
            def _():
                up.start()

        return begin

    end = BOTTOMS + nx * 96

    gather_half(0, 0, EXT, True)
    relay(0)
    z_copy(0, 4).start()
    z_copy(0, 5).start()
    gather_half(1, 0, EXT, True)
    lax.fori_loop(0, nx, near_cell, 0)
    near_products()
    relay(1)
    scatter(0, EXT // 2, 0, TOPS, True)
    forward(0)
    scatter(EXT // 2, EXT // 2, 0, TOPS, True)
    relay(2)
    arrived(0)
    for j, e in enumerate(far_cells):
        unpack_b(nx + j, e)
    forward(1)
    arrived(1)
    for j, e in enumerate(far_cells):
        unpack_a(nx + j, e)
        unpack_c(nx + j, e)
    far_bottoms()
    forward(2)
    for at in range(0, EXT, EXT // 2):
        scatter(at, EXT // 2, BOTTOMS, end, False)
    arrived(2)
    for j, e in enumerate(far_cells):
        unpack_d(nx + j, e)
    far_tops()
    begin_sums = start_both(sum_down, sum_up)
    for place in range(2):
        region = core if place == 0 else 1 - core
        scatter(pl.multiple_of(LOW + 2 * FACE * region, 2 * FACE), 2 * FACE, TOPS, BOTTOMS, False)
        begin_sums(place)
    scatter(0, INNER, TOPS, BOTTOMS, False)

    def keep_field(at, count, value):
        w = pl.ds(at, count)
        F[w, :] = value
        hi, lo = split(value)
        E[w, 0:COLS] = hi
        E[w, COLS : 2 * COLS] = lo

    def as_first(total, at, count):
        return (total - center * SX[pl.ds(at, count), :]) * (1.0 / half)

    keep_field(0, INNER, as_first(T[0:INNER], 0, INNER))
    gather(0, EARLY, True)

    def wait_for(region, from_low, from_high, buffer):
        low, high = region == 0, region == 1

        @pl.when(low & has_low)
        def _():
            from_low.wait_recv()

        @pl.when(high & has_high)
        def _():
            from_high.wait_recv()

        @pl.when((low & jnp.logical_not(has_low)) | (high & jnp.logical_not(has_high)))
        def _():
            buffer[region] = jnp.zeros(buffer.shape[1:], f32)

    for place in range(2):
        region = 1 - core if place == 0 else core
        wait_for(region, sum_up, sum_down, XR)
        for part in range(2):
            at = pl.multiple_of(LOW + 2 * FACE * region + FACE * part, FACE)
            total = T[pl.ds(at, FACE), :] + XR[region, FACE * part : FACE * (part + 1)]
            inside = (region == 1) | has_low if part == 0 else (region == 0) | has_high
            keep_field(at, FACE, jnp.where(inside, as_first(total, at, FACE), 0.0))
    gather(EARLY, EXT, False)

    near_products()
    far_products()

    @pl.when(has_low)
    def _():
        sum_down.wait_send()

    @pl.when(has_high)
    def _():
        sum_up.wait_send()

    begin_owned = start_both(own_down, own_up)
    for place in range(2):
        region = core if place == 0 else 1 - core
        scatter(pl.multiple_of(LOW + 3 * FACE * region, FACE), FACE, 0, end, True)
        begin_owned(place)

    def finish(i, to, at, count, total):
        part = pl.ds(to, count)
        O[part, :] = (total - center * F[pl.ds(at, count), :]) * (2.0 / half)
        store = pltpu.make_async_copy(O.at[part], out.at[part], local.at[i])
        store.start()
        return store

    scatter(0, INNER, 0, end, True)
    stores = [finish(0, FACE, 0, INNER, T[0:INNER])]
    scatter(LOW + FACE, 2 * FACE, 0, end, True)
    for place in range(2):
        region = 1 - core if place == 0 else core
        wait_for(region, own_up, own_down, YR)
        at = pl.multiple_of(LOW + FACE + FACE * region, FACE)
        to = pl.multiple_of((OWN - FACE) * region, FACE)
        stores.append(finish(1 + place, to, at, FACE, T[pl.ds(at, FACE), :] + YR[region]))

    for c in x_copies:
        c.wait_send()
    for k in range(len(PIECES)):
        z_copy(0, k).wait_send()
        z_copy(1, k).wait_send()
        for j, p in enumerate(xpeers):
            piece_copy(zpeer, k, p, f_send.at[k, j]).wait_send()

    @pl.when(has_low)
    def _():
        halo_down.wait_send()
        own_down.wait_send()

    @pl.when(has_high)
    def _():
        halo_up.wait_send()
        own_up.wait_send()

    for c in stores:
        c.wait()


def on_device(states, connectivity, cell_hamiltonian):
    anywhere = pl.BlockSpec(memory_space=pl.ANY)
    kt = CELLS * KC
    moved = pl.pallas_call(
        kernel,
        out_shape=jax.ShapeDtypeStruct((OWN, COLS), f32),
        in_specs=[anywhere] * 3,
        out_specs=anywhere,
        scratch_shapes=[
            pltpu.VMEM((kt, EXT), bf16),
            pltpu.VMEM((EXT, kt), bf16),
            pltpu.VMEM((CELLS, 2 * KC, 384), bf16),
            pltpu.VMEM((kt, 2 * COLS), bf16),
            pltpu.VMEM((kt, 2 * COLS), bf16),
            pltpu.VMEM((EXT, 2 * COLS), bf16),
            pltpu.VMEM((CELLS, PROWS, 128), f32),
            pltpu.VMEM((EXT, COLS), f32),
            pltpu.VMEM((EXT, COLS), f32),
            pltpu.VMEM((EXT, COLS), f32),
            pltpu.VMEM((2, 2 * FACE, COLS), f32),
            pltpu.VMEM((2, FACE, COLS), f32),
            pltpu.VMEM((KC, 384), f32),
            pltpu.VMEM((CELLS, 384), i32),
            pltpu.VMEM((1, kt), i32),
            pltpu.VMEM((CELLS, NPC), i32),
            pltpu.VMEM((NPC, 1, NPC), f32),
            pltpu.VMEM((OWN, COLS), f32),
            pltpu.VMEM((PROWS, 128), f32),
            pltpu.SemaphoreType.DMA((2, 6)),
            pltpu.SemaphoreType.DMA((2, 6)),
            pltpu.SemaphoreType.DMA((3,)),
            pltpu.SemaphoreType.DMA((6, 3)),
            pltpu.SemaphoreType.DMA((6,)),
            pltpu.SemaphoreType.DMA((CELLS, 6)),
            pltpu.SemaphoreType.DMA((6,)),
            pltpu.SemaphoreType.DMA((5,)),
        ],
        compiler_params=pltpu.CompilerParams(
            collective_id=0, has_side_effects=True, vmem_limit_bytes=58 << 20
        ),
    )(states, connectivity, cell_hamiltonian.reshape(NPC, 1, NPC))
    return moved - states


def solution(mesh):
    return jax.shard_map(
        on_device,
        mesh=mesh,
        in_specs=(P("domain", "band"), P("domain", None), P(("domain", "band"), None, None)),
        out_specs=P("domain", "band"),
        check_vma=False,
    )
```

```python
import functools

import jax
import jax.numpy as jnp
from jax import lax
from jax.experimental import pallas as pl
from jax.experimental.pallas import tpu as pltpu
from jax.sharding import PartitionSpec as P

MESH = pl.DeviceIdType.MESH
f32, bf16, i32, i16 = jnp.float32, jnp.bfloat16, jnp.int32, jnp.int16

NPC = 343
KC = 352
CELLS = 8
FACE = 288
OWN = 1728
EXT = OWN + 2 * FACE
COLS = 128
INNER = OWN - 2 * FACE

LOW = INNER
HIGH = INNER + 2 * FACE
EARLY = 1024

PB, PA, PC, PD, PROWS = 0, 176, 304, 352, 480
PIECES = ((0, 88), (88, 88), (176, 88), (264, 88), (352, 64), (416, 64))
HOP = 4

center = 0.5
half = 1.5


def split(value):
    hi = value.astype(bf16)
    lo = (value - hi.astype(f32)).astype(bf16)
    return hi, lo


def rows_cols(rows):
    return lax.broadcasted_iota(i32, (rows, 128), 0), lax.broadcasted_iota(i32, (rows, 128), 1)


def padded(value, count):
    return jnp.concatenate([value, jnp.zeros((count - value.shape[0], 128), f32)], axis=0)


def pack_corner(corner, roll):
    row, col = rows_cols(48)
    second = padded(roll(corner[48:88], 80), 48)
    both = jnp.where(row >= col, corner[0:48], second)
    diag = jnp.sum(jnp.where(row == col, second, 0.0), axis=1, keepdims=True)
    below = padded(corner[48:88], 48)
    packed = jnp.where(col < 48, below, jnp.where((col >= 64) & (col < 112), roll(both, 64), 0.0))
    return jnp.where(col == 127, diag, packed)


def unpack_corner(packed, roll):
    row, col = rows_cols(48)
    flipped = jnp.transpose(padded(packed, 128))
    both = roll(packed, 64)
    both_t = flipped[64:112]
    first = jnp.where(row >= col, both, both_t)
    second = jnp.where(row < col, both, jnp.where(row > col, both_t, packed[:, 127:128]))
    upper = jnp.where(col < 48, first, jnp.where(col < 88, roll(flipped[0:48], 48), 0.0))
    lower = jnp.where(col < 48, packed, jnp.where(col < 88, roll(second, 48), 0.0))
    return jnp.concatenate([upper, lower[0:40]], axis=0)


def lane_roll(value, shift):
    return pltpu.roll(value, shift, 1)


def kernel(
    states, conn, cell, out,
    G, S, Hs, X, PR, E, RX, T, SX, F, XR, YR, Hf, CP, CR, CN, V, O,
    RL, z_send, z_recv, x_send, f_send, n_send, cell_recv, n_recv, local,
):
    d = lax.axis_index("domain")
    b = lax.axis_index("band")
    last = lax.axis_size("domain") - 1
    nx = CELLS // 2
    xi = b // 2
    zh = b % 2
    zpeer = 2 * xi + 1 - zh
    xpeers = [2 * ((xi + j) % nx) + zh for j in (1, 3, 2)]
    z = 8 * zh + d // 8

    def along_z(way):
        to = (z + (HOP, 16 - HOP)[way]) % 16
        return (to % 8) * 8 + d % 8, 2 * xi + to // 8, to // 8

    has_low = d > 0
    has_high = d < last

    barrier = pltpu.get_barrier_semaphore()

    def greet(dd, bb):
        pl.semaphore_signal(barrier, inc=1, device_id=(dd, bb), device_id_type=MESH)

    for way in range(2):
        greet(*along_z(way)[:2])
    for p in xpeers:
        greet(d, p)

    @pl.when(has_low)
    def _():
        greet(d - 1, b)

    @pl.when(has_high)
    def _():
        greet(d + 1, b)

    load_cell = pltpu.make_async_copy(cell, V, local.at[0])
    load_conn = pltpu.make_async_copy(conn, CN, local.at[1])
    loads = [
        pltpu.make_async_copy(states.at[pl.ds(a, c)], SX.at[pl.ds(to, c)], local.at[2 + i])
        for i, (a, c, to) in enumerate(
            ((0, FACE, LOW + FACE), (OWN - FACE, FACE, HIGH), (FACE, INNER, 0))
        )
    ]
    for c in [load_cell, load_conn] + loads:
        c.start()

    Hf[...] = jnp.zeros_like(Hf)
    load_cell.wait()
    Hf[0:NPC, 0:NPC] = V[:, 0, :]
    row, col = rows_cols(128)
    row88 = rows_cols(88)[0]
    d2 = Hf[128:256, 128:256]
    diag = jnp.sum(jnp.where(row == col, d2, 0.0), axis=0, keepdims=True)
    RX[b, PB : PB + 88] = jnp.where(row88 == 87, diag, Hf[256:344, 0:128])
    RX[b, PB + 88 : PB + 176] = Hf[256:344, 128:256]
    RX[b, PA : PA + 128] = Hf[128:256, 0:128]
    RX[b, PD : PD + 128] = jnp.where(row >= col, Hf[0:128, 0:128], d2)
    RX[b, PC : PC + 48] = pack_corner(Hf[256:344, 256:384], lane_roll)

    pl.semaphore_wait(barrier, 5 + has_low.astype(i32) + has_high.astype(i32))

    def piece_copy(e, k, target, send_sem):
        part = RX.at[e, pl.ds(*PIECES[k])]
        return pltpu.make_async_remote_copy(
            src_ref=part, dst_ref=part, send_sem=send_sem, recv_sem=cell_recv.at[e, k],
            device_id=(d, target), device_id_type=MESH,
        )

    def whole_copy(e, target, send_sem):
        return pltpu.make_async_remote_copy(
            src_ref=RX.at[e], dst_ref=RX.at[e], send_sem=send_sem, recv_sem=cell_recv.at[e, 0],
            device_id=(d, target), device_id_type=MESH,
        )

    def node_copy(src, dst, i, dd):
        return pltpu.make_async_remote_copy(
            src_ref=src, dst_ref=dst, send_sem=n_send.at[i], recv_sem=n_recv.at[i],
            device_id=(dd, b), device_id_type=MESH,
        )

    def z_copy(leg, k):
        dd, bb, side = along_z(k % 2)
        rows = pl.ds(*PIECES[k])
        return pltpu.make_async_remote_copy(
            src_ref=RL.at[rows] if leg else RX.at[b, rows],
            dst_ref=RX.at[2 * xi + 1 - side, rows] if leg else RL.at[rows],
            send_sem=z_send.at[leg, k], recv_sem=z_recv.at[leg, k],
            device_id=(dd, bb), device_id_type=MESH,
        )

    for k in range(4):
        z_copy(0, k).start()
    x_copies = [whole_copy(b, p, x_send.at[j]) for j, p in enumerate(xpeers)]
    for c in x_copies:
        c.start()

    def exchange(step, down_src, down_dst, up_src, up_dst):
        down = node_copy(down_src, down_dst, 2 * step, d - 1)
        up = node_copy(up_src, up_dst, 2 * step + 1, d + 1)
        return down, up

    halo_down, halo_up = exchange(
        0, SX.at[pl.ds(LOW + FACE, FACE)], SX.at[pl.ds(HIGH + FACE, FACE)],
        SX.at[pl.ds(HIGH, FACE)], SX.at[pl.ds(LOW, FACE)],
    )
    sum_down, sum_up = exchange(
        1, T.at[pl.ds(LOW, 2 * FACE)], XR.at[1], T.at[pl.ds(HIGH, 2 * FACE)], XR.at[0]
    )
    own_down, own_up = exchange(
        2, T.at[pl.ds(LOW, FACE)], YR.at[1], T.at[pl.ds(HIGH + FACE, FACE)], YR.at[0]
    )

    loads[0].wait()
    loads[1].wait()

    @pl.when(has_low)
    def _():
        halo_down.start()

    @pl.when(has_high)
    def _():
        halo_up.start()

    CP[...] = jnp.full(CP.shape, -1, i32)
    load_conn.wait()
    n = CN[...]
    CP[:, 0:NPC] = jnp.where(n < 2 * FACE, n + LOW, jnp.where(n < OWN, n - 2 * FACE, n))

    def cell_of(s):
        side = s // nx
        return 2 * ((xi + s) % nx) + zh + side * (1 - 2 * zh)

    rows = [CP[pl.ds(cell_of(s), 1), :] for s in range(CELLS)]
    near = [r[:, :KC] for r in rows[:nx]]
    top = [r[:, :256] for r in rows[nx:]]
    bottom = [r[:, 256:KC] for r in rows[nx:]]
    CR[...] = jnp.concatenate(near + top + bottom, axis=1)

    def build_g(s, carry):
        line = jnp.broadcast_to(CP[pl.ds(cell_of(s), 1), :], (8, 384))
        column = jnp.transpose(line)[:KC, 0:1]
        wanted = jnp.broadcast_to(column, (KC, 128)).astype(i16)
        for j in range(EXT // 128):
            place = (lax.broadcasted_iota(i32, (KC, 128), 1) + j * 128).astype(i16)
            G[pl.ds(pl.multiple_of(s * KC, KC), KC), j * 128 : (j + 1) * 128] = jnp.where(
                wanted == place, bf16(1), bf16(0)
            )
        return carry

    lax.fori_loop(0, CELLS, build_g, 0)

    def build_s(j, carry):
        place = (lax.broadcasted_iota(i32, (256, 128), 0) + j * 256).astype(i16)
        for t in range(CELLS * KC // 128):
            wanted = jnp.broadcast_to(CR[0:1, t * 128 : (t + 1) * 128], (256, 128)).astype(i16)
            S[pl.ds(pl.multiple_of(j * 256, 256), 256), t * 128 : (t + 1) * 128] = jnp.where(
                wanted == place, bf16(1), bf16(0)
            )
        return carry

    lax.fori_loop(0, EXT // 256, build_s, 0)

    loads[2].wait()

    @pl.when(has_low)
    def _():
        halo_up.wait_recv()

    @pl.when(jnp.logical_not(has_low))
    def _():
        SX[LOW : LOW + FACE] = jnp.zeros((FACE, COLS), f32)

    @pl.when(has_high)
    def _():
        halo_down.wait_recv()

    @pl.when(jnp.logical_not(has_high))
    def _():
        SX[HIGH + FACE : EXT] = jnp.zeros((FACE, COLS), f32)

    def set_field(at, count, value):
        hi, lo = split(value)
        E[at : at + count, 0:COLS] = hi
        E[at : at + count, COLS : 2 * COLS] = lo

    set_field(0, EXT, SX[...])

    half_rows = CELLS * KC // 2

    def gather_half(m, start, stop, first):
        r = pl.ds(pl.multiple_of(m * half_rows, half_rows), half_rows)
        got = jnp.dot(G[r, start:stop], E[start:stop], preferred_element_type=f32)
        if not first:
            got = got + X[r, :].astype(f32)
        X[r, :] = got.astype(bf16)

    def gather(start, stop, first):
        def body(m, carry):
            gather_half(m, start, stop, first)
            return carry

        lax.fori_loop(0, 2, body, 0)

    def relay(group):
        for k in (2 * group, 2 * group + 1):
            z_copy(0, k).wait_recv()
            z_copy(1, k).start()

    def forward(group):
        for k in (2 * group, 2 * group + 1):
            z_copy(1, k).wait_recv()
            for j, p in enumerate(xpeers):
                piece_copy(zpeer, k, p, f_send.at[k, j]).start()

    def put(s, at, count, lane, value):
        hi, lo = split(value)
        base, step = (at, 256) if at < 256 else (512 + at - 256, 96)
        Hs[s, base : base + count, lane : lane + 128] = hi
        Hs[s, base + step : base + step + count, lane : lane + 128] = lo

    def unpack_b(s, e):
        for i in range(2):
            part = RX[e, PB + 88 * i : PB + 88 * (i + 1)]
            if i == 0:
                part = jnp.where(row88 == 87, 0.0, part)
            put(s, 256, 96, 128 * i, padded(part, 96))
            put(s, 128 * i, 128, 256, jnp.transpose(padded(part, 128)))

    def unpack_a(s, e):
        part = RX[e, PA : PA + 128]
        put(s, 128, 128, 0, part)
        put(s, 0, 128, 128, jnp.transpose(part))

    def unpack_d(s, e):
        part = RX[e, PD : PD + 128]
        flipped = jnp.transpose(part)
        middle = RX[e, PB + 87 : PB + 88]
        put(s, 0, 128, 0, jnp.where(row >= col, part, flipped))
        put(s, 128, 128, 128, jnp.where(row < col, part, jnp.where(row > col, flipped, middle)))

    def unpack_c(s, e):
        put(s, 256, 96, 256, padded(unpack_corner(RX[e, PC : PC + 48], lane_roll), 96))

    TOPS = nx * KC
    BOTTOMS = TOPS + nx * 256

    def product(s, base, count, *parts):
        t = jnp.dot(
            Hs[s, base : base + count, :KC], X[s * KC : (s + 1) * KC], preferred_element_type=f32
        )
        for at, rows, to in parts:
            hi_part, lo_part = t[at : at + rows], t[at + rows : at + 2 * rows]
            p = (lo_part[:, COLS:] + lo_part[:, :COLS]) + (hi_part[:, COLS:] + hi_part[:, :COLS])
            hi, lo = split(p)
            PR[to : to + rows, 0:COLS] = hi
            PR[to : to + rows, COLS : 2 * COLS] = lo

    def near_products():
        for j in range(nx):
            product(j, 0, 704, (0, 256, j * KC), (512, 96, j * KC + 256))

    def far_tops():
        for j in range(nx):
            product(nx + j, 0, 512, (0, 256, TOPS + j * 256))

    def far_bottoms():
        for j in range(nx):
            product(nx + j, 512, 192, (0, 96, BOTTOMS + j * 96))

    def far_products():
        for j in range(nx):
            product(nx + j, 0, 704, (0, 256, TOPS + j * 256), (512, 96, BOTTOMS + j * 96))

    def scatter(at, count, start, stop, first):
        w = pl.ds(at, count)
        got = jnp.dot(S[w, start:stop], PR[start:stop], preferred_element_type=f32)
        got = got[:, :COLS] + got[:, COLS:]
        T[w, :] = got if first else T[w, :] + got

    def near_cell(j, carry):
        e = cell_of(j)

        @pl.when(j > 0)
        def _():
            whole_copy(e, zpeer, x_send.at[0]).wait_recv()

        unpack_b(j, e)
        unpack_a(j, e)
        unpack_d(j, e)
        unpack_c(j, e)
        return carry

    far_cells = [cell_of(nx + j) for j in range(nx)]

    def arrived(group):
        for e in far_cells[1:]:
            for k in (2 * group, 2 * group + 1):
                piece_copy(e, k, zpeer, z_send.at[0, k]).wait_recv()

    core = d % 2
    down_first = core == 0

    def start_both(down, up):
        def begin(place):
            @pl.when(has_low & (down_first if place == 0 else jnp.logical_not(down_first)))
            def _():
                down.start()

            @pl.when(has_high & (jnp.logical_not(down_first) if place == 0 else down_first))
            def _():
                up.start()

        return begin

    end = BOTTOMS + nx * 96

    relay(0)
    z_copy(0, 4).start()
    z_copy(0, 5).start()
    gather_half(0, 0, EXT, True)
    gather_half(1, 0, EXT, True)
    relay(1)
    lax.fori_loop(0, nx, near_cell, 0)
    near_products()
    forward(0)
    relay(2)
    for at in range(0, EXT, EXT // 2):
        scatter(at, EXT // 2, 0, TOPS, True)
    forward(1)
    forward(2)
    arrived(0)
    for j, e in enumerate(far_cells):
        unpack_b(nx + j, e)
    arrived(1)
    for j, e in enumerate(far_cells):
        unpack_a(nx + j, e)
        unpack_c(nx + j, e)
    far_bottoms()
    for at in range(0, EXT, EXT // 2):
        scatter(at, EXT // 2, BOTTOMS, end, False)
    arrived(2)
    for j, e in enumerate(far_cells):
        unpack_d(nx + j, e)
    far_tops()
    begin_sums = start_both(sum_down, sum_up)
    for place in range(2):
        region = core if place == 0 else 1 - core
        scatter(pl.multiple_of(LOW + 2 * FACE * region, 2 * FACE), 2 * FACE, TOPS, BOTTOMS, False)
        begin_sums(place)
    scatter(0, INNER, TOPS, BOTTOMS, False)

    def keep_field(at, count, value):
        w = pl.ds(at, count)
        F[w, :] = value
        hi, lo = split(value)
        E[w, 0:COLS] = hi
        E[w, COLS : 2 * COLS] = lo

    def as_first(total, at, count):
        return (total - center * SX[pl.ds(at, count), :]) * (1.0 / half)

    keep_field(0, INNER, as_first(T[0:INNER], 0, INNER))
    gather(0, EARLY, True)

    def wait_for(region, from_low, from_high, buffer):
        low, high = region == 0, region == 1

        @pl.when(low & has_low)
        def _():
            from_low.wait_recv()

        @pl.when(high & has_high)
        def _():
            from_high.wait_recv()

        @pl.when((low & jnp.logical_not(has_low)) | (high & jnp.logical_not(has_high)))
        def _():
            buffer[region] = jnp.zeros(buffer.shape[1:], f32)

    for place in range(2):
        region = 1 - core if place == 0 else core
        wait_for(region, sum_up, sum_down, XR)
        for part in range(2):
            at = pl.multiple_of(LOW + 2 * FACE * region + FACE * part, FACE)
            total = T[pl.ds(at, FACE), :] + XR[region, FACE * part : FACE * (part + 1)]
            inside = (region == 1) | has_low if part == 0 else (region == 0) | has_high
            keep_field(at, FACE, jnp.where(inside, as_first(total, at, FACE), 0.0))
    gather(EARLY, EXT, False)

    near_products()
    far_products()

    @pl.when(has_low)
    def _():
        sum_down.wait_send()

    @pl.when(has_high)
    def _():
        sum_up.wait_send()

    begin_owned = start_both(own_down, own_up)
    for place in range(2):
        region = core if place == 0 else 1 - core
        scatter(pl.multiple_of(LOW + 3 * FACE * region, FACE), FACE, 0, end, True)
        begin_owned(place)

    def finish(i, to, at, count, total):
        part = pl.ds(to, count)
        O[part, :] = (total - center * F[pl.ds(at, count), :]) * (2.0 / half)
        store = pltpu.make_async_copy(O.at[part], out.at[part], local.at[i])
        store.start()
        return store

    scatter(0, INNER, 0, end, True)
    stores = [finish(0, FACE, 0, INNER, T[0:INNER])]
    scatter(LOW + FACE, 2 * FACE, 0, end, True)
    for place in range(2):
        region = 1 - core if place == 0 else core
        wait_for(region, own_up, own_down, YR)
        at = pl.multiple_of(LOW + FACE + FACE * region, FACE)
        to = pl.multiple_of((OWN - FACE) * region, FACE)
        stores.append(finish(1 + place, to, at, FACE, T[pl.ds(at, FACE), :] + YR[region]))

    for c in x_copies:
        c.wait_send()
    for k in range(len(PIECES)):
        z_copy(0, k).wait_send()
        z_copy(1, k).wait_send()
        for j, p in enumerate(xpeers):
            piece_copy(zpeer, k, p, f_send.at[k, j]).wait_send()

    @pl.when(has_low)
    def _():
        halo_down.wait_send()
        own_down.wait_send()

    @pl.when(has_high)
    def _():
        halo_up.wait_send()
        own_up.wait_send()

    for c in stores:
        c.wait()


def on_device(states, connectivity, cell_hamiltonian):
    anywhere = pl.BlockSpec(memory_space=pl.ANY)
    kt = CELLS * KC
    moved = pl.pallas_call(
        kernel,
        out_shape=jax.ShapeDtypeStruct((OWN, COLS), f32),
        in_specs=[anywhere] * 3,
        out_specs=anywhere,
        scratch_shapes=[
            pltpu.VMEM((kt, EXT), bf16),
            pltpu.VMEM((EXT, kt), bf16),
            pltpu.VMEM((CELLS, 2 * KC, 384), bf16),
            pltpu.VMEM((kt, 2 * COLS), bf16),
            pltpu.VMEM((kt, 2 * COLS), bf16),
            pltpu.VMEM((EXT, 2 * COLS), bf16),
            pltpu.VMEM((CELLS, PROWS, 128), f32),
            pltpu.VMEM((EXT, COLS), f32),
            pltpu.VMEM((EXT, COLS), f32),
            pltpu.VMEM((EXT, COLS), f32),
            pltpu.VMEM((2, 2 * FACE, COLS), f32),
            pltpu.VMEM((2, FACE, COLS), f32),
            pltpu.VMEM((KC, 384), f32),
            pltpu.VMEM((CELLS, 384), i32),
            pltpu.VMEM((1, kt), i32),
            pltpu.VMEM((CELLS, NPC), i32),
            pltpu.VMEM((NPC, 1, NPC), f32),
            pltpu.VMEM((OWN, COLS), f32),
            pltpu.VMEM((PROWS, 128), f32),
            pltpu.SemaphoreType.DMA((2, 6)),
            pltpu.SemaphoreType.DMA((2, 6)),
            pltpu.SemaphoreType.DMA((3,)),
            pltpu.SemaphoreType.DMA((6, 3)),
            pltpu.SemaphoreType.DMA((6,)),
            pltpu.SemaphoreType.DMA((CELLS, 6)),
            pltpu.SemaphoreType.DMA((6,)),
            pltpu.SemaphoreType.DMA((5,)),
        ],
        compiler_params=pltpu.CompilerParams(
            collective_id=0, has_side_effects=True, vmem_limit_bytes=58 << 20
        ),
    )(states, connectivity, cell_hamiltonian.reshape(NPC, 1, NPC))
    return moved - states


def solution(mesh):
    return jax.shard_map(
        on_device,
        mesh=mesh,
        in_specs=(P("domain", "band"), P("domain", None), P(("domain", "band"), None, None)),
        out_specs=P("domain", "band"),
        check_vma=False,
    )
```

```python
import functools

import jax
import jax.numpy as jnp
from jax import lax
from jax.experimental import pallas as pl
from jax.experimental.pallas import tpu as pltpu
from jax.sharding import PartitionSpec as P

MESH = pl.DeviceIdType.MESH
f32, bf16, i32, i16 = jnp.float32, jnp.bfloat16, jnp.int32, jnp.int16

NPC = 343
KC = 352
CELLS = 8
FACE = 288
OWN = 1728
EXT = OWN + 2 * FACE
COLS = 128
INNER = OWN - 2 * FACE

LOW = INNER
HIGH = INNER + 2 * FACE
EARLY = 1024

PB, PA, PC, PD, PROWS = 0, 176, 304, 352, 480
PIECES = ((0, 88), (88, 88), (176, 88), (264, 88), (352, 64), (416, 64))
HOP = 4

center = 0.5
half = 1.5


def split(value):
    hi = value.astype(bf16)
    lo = (value - hi.astype(f32)).astype(bf16)
    return hi, lo


def rows_cols(rows):
    return lax.broadcasted_iota(i32, (rows, 128), 0), lax.broadcasted_iota(i32, (rows, 128), 1)


def padded(value, count):
    return jnp.concatenate([value, jnp.zeros((count - value.shape[0], 128), f32)], axis=0)


def pack_corner(corner, roll):
    row, col = rows_cols(48)
    second = padded(roll(corner[48:88], 80), 48)
    both = jnp.where(row >= col, corner[0:48], second)
    diag = jnp.sum(jnp.where(row == col, second, 0.0), axis=1, keepdims=True)
    below = padded(corner[48:88], 48)
    packed = jnp.where(col < 48, below, jnp.where((col >= 64) & (col < 112), roll(both, 64), 0.0))
    return jnp.where(col == 127, diag, packed)


def unpack_corner(packed, roll):
    row, col = rows_cols(48)
    flipped = jnp.transpose(padded(packed, 128))
    both = roll(packed, 64)
    both_t = flipped[64:112]
    first = jnp.where(row >= col, both, both_t)
    second = jnp.where(row < col, both, jnp.where(row > col, both_t, packed[:, 127:128]))
    upper = jnp.where(col < 48, first, jnp.where(col < 88, roll(flipped[0:48], 48), 0.0))
    lower = jnp.where(col < 48, packed, jnp.where(col < 88, roll(second, 48), 0.0))
    return jnp.concatenate([upper, lower[0:40]], axis=0)


def lane_roll(value, shift):
    return pltpu.roll(value, shift, 1)


def kernel(
    states, conn, cell, out,
    G, S, Hs, X, PR, E, RX, T, SX, F, XR, YR, Hf, CP, CR, CN, V,
    RL, z_send, z_recv, x_send, f_send, n_send, cell_recv, n_recv, local,
):
    d = lax.axis_index("domain")
    b = lax.axis_index("band")
    last = lax.axis_size("domain") - 1
    nx = CELLS // 2
    xi = b // 2
    zh = b % 2
    zpeer = 2 * xi + 1 - zh
    xpeers = [2 * ((xi + j) % nx) + zh for j in (2, 1, 3)]
    z = 8 * zh + d // 8

    def along_z(way):
        to = (z + (HOP, 16 - HOP)[way]) % 16
        return (to % 8) * 8 + d % 8, 2 * xi + to // 8, to // 8

    has_low = d > 0
    has_high = d < last

    barrier = pltpu.get_barrier_semaphore()

    def greet(dd, bb):
        pl.semaphore_signal(barrier, inc=1, device_id=(dd, bb), device_id_type=MESH)

    for way in range(2):
        greet(*along_z(way)[:2])
    for p in xpeers:
        greet(d, p)

    @pl.when(has_low)
    def _():
        greet(d - 1, b)

    @pl.when(has_high)
    def _():
        greet(d + 1, b)

    load_cell = pltpu.make_async_copy(cell, V, local.at[0])
    load_conn = pltpu.make_async_copy(conn, CN, local.at[1])
    loads = [
        pltpu.make_async_copy(states.at[pl.ds(a, c)], SX.at[pl.ds(to, c)], local.at[2 + i])
        for i, (a, c, to) in enumerate(
            ((0, FACE, LOW + FACE), (OWN - FACE, FACE, HIGH), (FACE, INNER, 0))
        )
    ]
    for c in [load_cell, load_conn] + loads:
        c.start()

    Hf[...] = jnp.zeros_like(Hf)
    load_cell.wait()
    Hf[0:NPC, 0:NPC] = V[:, 0, :]
    row, col = rows_cols(128)
    row88 = rows_cols(88)[0]
    d2 = Hf[128:256, 128:256]
    diag = jnp.sum(jnp.where(row == col, d2, 0.0), axis=0, keepdims=True)
    RX[b, PB : PB + 88] = jnp.where(row88 == 87, diag, Hf[256:344, 0:128])
    RX[b, PB + 88 : PB + 176] = Hf[256:344, 128:256]
    RX[b, PA : PA + 128] = Hf[128:256, 0:128]
    RX[b, PD : PD + 128] = jnp.where(row >= col, Hf[0:128, 0:128], d2)
    RX[b, PC : PC + 48] = pack_corner(Hf[256:344, 256:384], lane_roll)

    pl.semaphore_wait(barrier, 5 + has_low.astype(i32) + has_high.astype(i32))

    def piece_copy(e, k, target, send_sem):
        part = RX.at[e, pl.ds(*PIECES[k])]
        return pltpu.make_async_remote_copy(
            src_ref=part, dst_ref=part, send_sem=send_sem, recv_sem=cell_recv.at[e, k],
            device_id=(d, target), device_id_type=MESH,
        )

    def whole_copy(e, target, send_sem):
        return pltpu.make_async_remote_copy(
            src_ref=RX.at[e], dst_ref=RX.at[e], send_sem=send_sem, recv_sem=cell_recv.at[e, 0],
            device_id=(d, target), device_id_type=MESH,
        )

    def node_copy(src, dst, i, dd):
        return pltpu.make_async_remote_copy(
            src_ref=src, dst_ref=dst, send_sem=n_send.at[i], recv_sem=n_recv.at[i],
            device_id=(dd, b), device_id_type=MESH,
        )

    def z_copy(leg, k):
        dd, bb, side = along_z(k % 2)
        rows = pl.ds(*PIECES[k])
        return pltpu.make_async_remote_copy(
            src_ref=RL.at[rows] if leg else RX.at[b, rows],
            dst_ref=RX.at[2 * xi + 1 - side, rows] if leg else RL.at[rows],
            send_sem=z_send.at[leg, k], recv_sem=z_recv.at[leg, k],
            device_id=(dd, bb), device_id_type=MESH,
        )

    for k in range(4):
        z_copy(0, k).start()
    x_copies = [whole_copy(b, p, x_send.at[j]) for j, p in enumerate(xpeers)]
    for c in x_copies:
        c.start()

    def exchange(step, down_src, down_dst, up_src, up_dst):
        down = node_copy(down_src, down_dst, 2 * step, d - 1)
        up = node_copy(up_src, up_dst, 2 * step + 1, d + 1)
        return down, up

    halo_down, halo_up = exchange(
        0, SX.at[pl.ds(LOW + FACE, FACE)], SX.at[pl.ds(HIGH + FACE, FACE)],
        SX.at[pl.ds(HIGH, FACE)], SX.at[pl.ds(LOW, FACE)],
    )
    sum_down, sum_up = exchange(
        1, T.at[pl.ds(LOW, 2 * FACE)], XR.at[1], T.at[pl.ds(HIGH, 2 * FACE)], XR.at[0]
    )
    own_down, own_up = exchange(
        2, T.at[pl.ds(LOW, FACE)], YR.at[1], T.at[pl.ds(HIGH + FACE, FACE)], YR.at[0]
    )

    loads[0].wait()
    loads[1].wait()

    @pl.when(has_low)
    def _():
        halo_down.start()

    @pl.when(has_high)
    def _():
        halo_up.start()

    CP[...] = jnp.full(CP.shape, -1, i32)
    load_conn.wait()
    n = CN[...]
    CP[:, 0:NPC] = jnp.where(n < 2 * FACE, n + LOW, jnp.where(n < OWN, n - 2 * FACE, n))

    def cell_of(s):
        side = s // nx
        return 2 * ((xi + s) % nx) + zh + side * (1 - 2 * zh)

    rows = [CP[pl.ds(cell_of(s), 1), :] for s in range(CELLS)]
    near = [r[:, :KC] for r in rows[:nx]]
    top = [r[:, :256] for r in rows[nx:]]
    bottom = [r[:, 256:KC] for r in rows[nx:]]
    CR[...] = jnp.concatenate(near + top + bottom, axis=1)

    def build_g(s, carry):
        line = jnp.broadcast_to(CP[pl.ds(cell_of(s), 1), :], (8, 384))
        column = jnp.transpose(line)[:KC, 0:1]
        wanted = jnp.broadcast_to(column, (KC, 128)).astype(i16)
        for j in range(EXT // 128):
            place = (lax.broadcasted_iota(i32, (KC, 128), 1) + j * 128).astype(i16)
            G[pl.ds(pl.multiple_of(s * KC, KC), KC), j * 128 : (j + 1) * 128] = jnp.where(
                wanted == place, bf16(1), bf16(0)
            )
        return carry

    lax.fori_loop(0, CELLS, build_g, 0)

    def build_s(j, carry):
        place = (lax.broadcasted_iota(i32, (256, 128), 0) + j * 256).astype(i16)
        for t in range(CELLS * KC // 128):
            wanted = jnp.broadcast_to(CR[0:1, t * 128 : (t + 1) * 128], (256, 128)).astype(i16)
            S[pl.ds(pl.multiple_of(j * 256, 256), 256), t * 128 : (t + 1) * 128] = jnp.where(
                wanted == place, bf16(1), bf16(0)
            )
        return carry

    lax.fori_loop(0, EXT // 256, build_s, 0)

    loads[2].wait()

    @pl.when(has_low)
    def _():
        halo_up.wait_recv()

    @pl.when(jnp.logical_not(has_low))
    def _():
        SX[LOW : LOW + FACE] = jnp.zeros((FACE, COLS), f32)

    @pl.when(has_high)
    def _():
        halo_down.wait_recv()

    @pl.when(jnp.logical_not(has_high))
    def _():
        SX[HIGH + FACE : EXT] = jnp.zeros((FACE, COLS), f32)

    def set_field(at, count, value):
        hi, lo = split(value)
        E[at : at + count, 0:COLS] = hi
        E[at : at + count, COLS : 2 * COLS] = lo

    set_field(0, EXT, SX[...])

    half_rows = CELLS * KC // 2

    def gather_half(m, start, stop, first):
        r = pl.ds(pl.multiple_of(m * half_rows, half_rows), half_rows)
        got = jnp.dot(G[r, start:stop], E[start:stop], preferred_element_type=f32)
        if not first:
            got = got + X[r, :].astype(f32)
        X[r, :] = got.astype(bf16)

    def gather(start, stop, first):
        def body(m, carry):
            gather_half(m, start, stop, first)
            return carry

        lax.fori_loop(0, 2, body, 0)

    def relay(group):
        for k in (2 * group, 2 * group + 1):
            z_copy(0, k).wait_recv()
            z_copy(1, k).start()

    def forward(group):
        for k in (2 * group, 2 * group + 1):
            z_copy(1, k).wait_recv()
            for j, p in enumerate(xpeers):
                piece_copy(zpeer, k, p, f_send.at[k, j]).start()

    def put(s, at, count, lane, value):
        hi, lo = split(value)
        base, step = (at, 256) if at < 256 else (512 + at - 256, 96)
        Hs[s, base : base + count, lane : lane + 128] = hi
        Hs[s, base + step : base + step + count, lane : lane + 128] = lo

    def unpack_b(s, e):
        for i in range(2):
            part = RX[e, PB + 88 * i : PB + 88 * (i + 1)]
            if i == 0:
                part = jnp.where(row88 == 87, 0.0, part)
            put(s, 256, 96, 128 * i, padded(part, 96))
            put(s, 128 * i, 128, 256, jnp.transpose(padded(part, 128)))

    def unpack_a(s, e):
        part = RX[e, PA : PA + 128]
        put(s, 128, 128, 0, part)
        put(s, 0, 128, 128, jnp.transpose(part))

    def unpack_d(s, e):
        part = RX[e, PD : PD + 128]
        flipped = jnp.transpose(part)
        middle = RX[e, PB + 87 : PB + 88]
        put(s, 0, 128, 0, jnp.where(row >= col, part, flipped))
        put(s, 128, 128, 128, jnp.where(row < col, part, jnp.where(row > col, flipped, middle)))

    def unpack_c(s, e):
        put(s, 256, 96, 256, padded(unpack_corner(RX[e, PC : PC + 48], lane_roll), 96))

    TOPS = nx * KC
    BOTTOMS = TOPS + nx * 256

    def product(s, base, count, *parts):
        t = jnp.dot(
            Hs[s, base : base + count, :KC], X[s * KC : (s + 1) * KC], preferred_element_type=f32
        )
        for at, rows, to in parts:
            hi_part, lo_part = t[at : at + rows], t[at + rows : at + 2 * rows]
            p = (lo_part[:, COLS:] + lo_part[:, :COLS]) + (hi_part[:, COLS:] + hi_part[:, :COLS])
            hi, lo = split(p)
            PR[to : to + rows, 0:COLS] = hi
            PR[to : to + rows, COLS : 2 * COLS] = lo

    def near_products():
        for j in range(nx):
            product(j, 0, 704, (0, 256, j * KC), (512, 96, j * KC + 256))

    def far_tops():
        for j in range(nx):
            product(nx + j, 0, 512, (0, 256, TOPS + j * 256))

    def far_bottoms():
        for j in range(nx):
            product(nx + j, 512, 192, (0, 96, BOTTOMS + j * 96))

    def far_products():
        for j in range(nx):
            product(nx + j, 0, 704, (0, 256, TOPS + j * 256), (512, 96, BOTTOMS + j * 96))

    def scatter(at, count, start, stop, first):
        w = pl.ds(at, count)
        got = jnp.dot(S[w, start:stop], PR[start:stop], preferred_element_type=f32)
        got = got[:, :COLS] + got[:, COLS:]
        T[w, :] = got if first else T[w, :] + got

    def near_cell(j, carry):
        e = cell_of(j)

        @pl.when(j > 0)
        def _():
            whole_copy(e, zpeer, x_send.at[0]).wait_recv()

        unpack_b(j, e)
        unpack_a(j, e)
        unpack_d(j, e)
        unpack_c(j, e)
        return carry

    far_cells = [cell_of(nx + j) for j in range(nx)]

    def arrived(group):
        for e in far_cells[1:]:
            for k in (2 * group, 2 * group + 1):
                piece_copy(e, k, zpeer, z_send.at[0, k]).wait_recv()

    core = d % 2
    down_first = core == 0

    def start_both(down, up):
        def begin(place):
            @pl.when(has_low & (down_first if place == 0 else jnp.logical_not(down_first)))
            def _():
                down.start()

            @pl.when(has_high & (jnp.logical_not(down_first) if place == 0 else down_first))
            def _():
                up.start()

        return begin

    end = BOTTOMS + nx * 96

    relay(0)
    z_copy(0, 4).start()
    z_copy(0, 5).start()
    gather_half(0, 0, EXT, True)
    gather_half(1, 0, EXT, True)
    relay(1)
    lax.fori_loop(0, nx, near_cell, 0)
    near_products()
    forward(0)
    relay(2)
    for at in range(0, EXT, EXT // 2):
        scatter(at, EXT // 2, 0, TOPS, True)
    forward(1)
    forward(2)
    arrived(0)
    for j, e in enumerate(far_cells):
        unpack_b(nx + j, e)
    arrived(1)
    for j, e in enumerate(far_cells):
        unpack_a(nx + j, e)
        unpack_c(nx + j, e)
    far_bottoms()
    for at in range(0, EXT, EXT // 2):
        scatter(at, EXT // 2, BOTTOMS, end, False)
    arrived(2)
    for j, e in enumerate(far_cells):
        unpack_d(nx + j, e)
    far_tops()
    begin_sums = start_both(sum_down, sum_up)
    for place in range(2):
        region = core if place == 0 else 1 - core
        scatter(pl.multiple_of(LOW + 2 * FACE * region, 2 * FACE), 2 * FACE, TOPS, BOTTOMS, False)
        begin_sums(place)
    scatter(0, INNER, TOPS, BOTTOMS, False)

    def keep_field(at, count, value):
        w = pl.ds(at, count)
        F[w, :] = value
        hi, lo = split(value)
        E[w, 0:COLS] = hi
        E[w, COLS : 2 * COLS] = lo

    def as_first(total, at, count):
        return (total - center * SX[pl.ds(at, count), :]) * (1.0 / half)

    keep_field(0, INNER, as_first(T[0:INNER], 0, INNER))
    gather(0, EARLY, True)

    def wait_for(region, from_low, from_high, buffer):
        low, high = region == 0, region == 1

        @pl.when(low & has_low)
        def _():
            from_low.wait_recv()

        @pl.when(high & has_high)
        def _():
            from_high.wait_recv()

        @pl.when((low & jnp.logical_not(has_low)) | (high & jnp.logical_not(has_high)))
        def _():
            buffer[region] = jnp.zeros(buffer.shape[1:], f32)

    for place in range(2):
        region = 1 - core if place == 0 else core
        wait_for(region, sum_up, sum_down, XR)
        for part in range(2):
            at = pl.multiple_of(LOW + 2 * FACE * region + FACE * part, FACE)
            total = T[pl.ds(at, FACE), :] + XR[region, FACE * part : FACE * (part + 1)]
            inside = (region == 1) | has_low if part == 0 else (region == 0) | has_high
            keep_field(at, FACE, jnp.where(inside, as_first(total, at, FACE), 0.0))
    gather(EARLY, EXT, False)

    near_products()
    far_products()

    @pl.when(has_low)
    def _():
        sum_down.wait_send()

    @pl.when(has_high)
    def _():
        sum_up.wait_send()

    begin_owned = start_both(own_down, own_up)
    for place in range(2):
        region = core if place == 0 else 1 - core
        scatter(pl.multiple_of(LOW + 3 * FACE * region, FACE), FACE, 0, end, True)
        begin_owned(place)

    def finish(i, to, at, count, total):
        part = pl.ds(to, count)
        out[part, :] = (total - center * F[pl.ds(at, count), :]) * (2.0 / half)

    scatter(0, INNER, 0, end, True)
    finish(0, FACE, 0, INNER, T[0:INNER])
    scatter(LOW + FACE, 2 * FACE, 0, end, True)
    for place in range(2):
        region = 1 - core if place == 0 else core
        wait_for(region, own_up, own_down, YR)
        at = pl.multiple_of(LOW + FACE + FACE * region, FACE)
        to = pl.multiple_of((OWN - FACE) * region, FACE)
        finish(1 + place, to, at, FACE, T[pl.ds(at, FACE), :] + YR[region])

    for c in x_copies:
        c.wait_send()
    for k in range(len(PIECES)):
        z_copy(0, k).wait_send()
        z_copy(1, k).wait_send()
        for j, p in enumerate(xpeers):
            piece_copy(zpeer, k, p, f_send.at[k, j]).wait_send()

    @pl.when(has_low)
    def _():
        halo_down.wait_send()
        own_down.wait_send()

    @pl.when(has_high)
    def _():
        halo_up.wait_send()
        own_up.wait_send()


def on_device(states, connectivity, cell_hamiltonian):
    anywhere = pl.BlockSpec(memory_space=pl.ANY)
    kt = CELLS * KC
    moved = pl.pallas_call(
        kernel,
        out_shape=pltpu.VMEM((OWN, COLS), f32),
        in_specs=[anywhere] * 3,
        out_specs=pl.BlockSpec(memory_space=pltpu.VMEM),
        scratch_shapes=[
            pltpu.VMEM((kt, EXT), bf16),
            pltpu.VMEM((EXT, kt), bf16),
            pltpu.VMEM((CELLS, 2 * KC, 384), bf16),
            pltpu.VMEM((kt, 2 * COLS), bf16),
            pltpu.VMEM((kt, 2 * COLS), bf16),
            pltpu.VMEM((EXT, 2 * COLS), bf16),
            pltpu.VMEM((CELLS, PROWS, 128), f32),
            pltpu.VMEM((EXT, COLS), f32),
            pltpu.VMEM((EXT, COLS), f32),
            pltpu.VMEM((EXT, COLS), f32),
            pltpu.VMEM((2, 2 * FACE, COLS), f32),
            pltpu.VMEM((2, FACE, COLS), f32),
            pltpu.VMEM((KC, 384), f32),
            pltpu.VMEM((CELLS, 384), i32),
            pltpu.VMEM((1, kt), i32),
            pltpu.VMEM((CELLS, NPC), i32),
            pltpu.VMEM((NPC, 1, NPC), f32),
            pltpu.VMEM((PROWS, 128), f32),
            pltpu.SemaphoreType.DMA((2, 6)),
            pltpu.SemaphoreType.DMA((2, 6)),
            pltpu.SemaphoreType.DMA((3,)),
            pltpu.SemaphoreType.DMA((6, 3)),
            pltpu.SemaphoreType.DMA((6,)),
            pltpu.SemaphoreType.DMA((CELLS, 6)),
            pltpu.SemaphoreType.DMA((6,)),
            pltpu.SemaphoreType.DMA((5,)),
        ],
        compiler_params=pltpu.CompilerParams(
            collective_id=0, has_side_effects=True, vmem_limit_bytes=58 << 20
        ),
    )(states, connectivity, cell_hamiltonian.reshape(NPC, 1, NPC))
    return moved - states


def solution(mesh):
    return jax.shard_map(
        on_device,
        mesh=mesh,
        in_specs=(P("domain", "band"), P("domain", None), P(("domain", "band"), None, None)),
        out_specs=P("domain", "band"),
        check_vma=False,
    )
```

```python
import functools

import jax
import jax.numpy as jnp
from jax import lax
from jax.experimental import pallas as pl
from jax.experimental.pallas import tpu as pltpu
from jax.sharding import PartitionSpec as P

MESH = pl.DeviceIdType.MESH
f32, bf16, i32, i16 = jnp.float32, jnp.bfloat16, jnp.int32, jnp.int16

NPC = 343
KC = 352
CELLS = 8
FACE = 288
OWN = 1728
EXT = OWN + 2 * FACE
COLS = 128
INNER = OWN - 2 * FACE

LOW = INNER
HIGH = INNER + 2 * FACE
EARLY = 1024

PB, PA, PC, PD, PROWS = 0, 176, 304, 352, 480
PIECES = ((0, 88), (88, 88), (176, 88), (264, 88), (352, 64), (416, 64))
HOP = 4

center = 0.5
half = 1.5


def split(value):
    hi = value.astype(bf16)
    lo = (value - hi.astype(f32)).astype(bf16)
    return hi, lo


def rows_cols(rows):
    return lax.broadcasted_iota(i32, (rows, 128), 0), lax.broadcasted_iota(i32, (rows, 128), 1)


def padded(value, count):
    return jnp.concatenate([value, jnp.zeros((count - value.shape[0], 128), f32)], axis=0)


def pack_corner(corner, roll):
    row, col = rows_cols(48)
    second = padded(roll(corner[48:88], 80), 48)
    both = jnp.where(row >= col, corner[0:48], second)
    diag = jnp.sum(jnp.where(row == col, second, 0.0), axis=1, keepdims=True)
    below = padded(corner[48:88], 48)
    packed = jnp.where(col < 48, below, jnp.where((col >= 64) & (col < 112), roll(both, 64), 0.0))
    return jnp.where(col == 127, diag, packed)


def unpack_corner(packed, roll):
    row, col = rows_cols(48)
    flipped = jnp.transpose(padded(packed, 128))
    both = roll(packed, 64)
    both_t = flipped[64:112]
    first = jnp.where(row >= col, both, both_t)
    second = jnp.where(row < col, both, jnp.where(row > col, both_t, packed[:, 127:128]))
    upper = jnp.where(col < 48, first, jnp.where(col < 88, roll(flipped[0:48], 48), 0.0))
    lower = jnp.where(col < 48, packed, jnp.where(col < 88, roll(second, 48), 0.0))
    return jnp.concatenate([upper, lower[0:40]], axis=0)


def lane_roll(value, shift):
    return pltpu.roll(value, shift, 1)


def kernel(
    states, conn, cell, out,
    G, S, Hs, X, PR, E, RX, T, SX, F, XR, YR, Hf, CP, CR, CN, V,
    RL, z_send, z_recv, x_send, f_send, n_send, cell_recv, n_recv, local,
):
    d = lax.axis_index("domain")
    b = lax.axis_index("band")
    last = lax.axis_size("domain") - 1
    nx = CELLS // 2
    xi = b // 2
    zh = b % 2
    zpeer = 2 * xi + 1 - zh
    xpeers = [2 * ((xi + j) % nx) + zh for j in (2, 1, 3)]
    z = 8 * zh + d // 8

    def along_z(way):
        to = (z + (HOP, 16 - HOP)[way]) % 16
        return (to % 8) * 8 + d % 8, 2 * xi + to // 8, to // 8

    has_low = d > 0
    has_high = d < last

    barrier = pltpu.get_barrier_semaphore()

    def greet(dd, bb):
        pl.semaphore_signal(barrier, inc=1, device_id=(dd, bb), device_id_type=MESH)

    for way in range(2):
        greet(*along_z(way)[:2])
    for p in xpeers:
        greet(d, p)

    @pl.when(has_low)
    def _():
        greet(d - 1, b)

    @pl.when(has_high)
    def _():
        greet(d + 1, b)

    load_cell = pltpu.make_async_copy(cell, V, local.at[0])
    load_conn = pltpu.make_async_copy(conn, CN, local.at[1])
    loads = [
        pltpu.make_async_copy(states.at[pl.ds(a, c)], SX.at[pl.ds(to, c)], local.at[2 + i])
        for i, (a, c, to) in enumerate(
            ((0, FACE, LOW + FACE), (OWN - FACE, FACE, HIGH), (FACE, INNER, 0))
        )
    ]
    for c in [load_cell, load_conn] + loads:
        c.start()

    Hf[...] = jnp.zeros_like(Hf)
    load_cell.wait()
    Hf[0:NPC, 0:NPC] = V[:, 0, :]
    row, col = rows_cols(128)
    row88 = rows_cols(88)[0]
    d2 = Hf[128:256, 128:256]
    diag = jnp.sum(jnp.where(row == col, d2, 0.0), axis=0, keepdims=True)
    RX[b, PB : PB + 88] = jnp.where(row88 == 87, diag, Hf[256:344, 0:128])
    RX[b, PB + 88 : PB + 176] = Hf[256:344, 128:256]
    RX[b, PA : PA + 128] = Hf[128:256, 0:128]
    RX[b, PD : PD + 128] = jnp.where(row >= col, Hf[0:128, 0:128], d2)
    RX[b, PC : PC + 48] = pack_corner(Hf[256:344, 256:384], lane_roll)

    pl.semaphore_wait(barrier, 5 + has_low.astype(i32) + has_high.astype(i32))

    def piece_copy(e, k, target, send_sem):
        part = RX.at[e, pl.ds(*PIECES[k])]
        return pltpu.make_async_remote_copy(
            src_ref=part, dst_ref=part, send_sem=send_sem, recv_sem=cell_recv.at[e, k],
            device_id=(d, target), device_id_type=MESH,
        )

    def whole_copy(e, target, send_sem):
        return pltpu.make_async_remote_copy(
            src_ref=RX.at[e], dst_ref=RX.at[e], send_sem=send_sem, recv_sem=cell_recv.at[e, 0],
            device_id=(d, target), device_id_type=MESH,
        )

    def node_copy(src, dst, i, dd):
        return pltpu.make_async_remote_copy(
            src_ref=src, dst_ref=dst, send_sem=n_send.at[i], recv_sem=n_recv.at[i],
            device_id=(dd, b), device_id_type=MESH,
        )

    def z_copy(leg, k):
        dd, bb, side = along_z(k % 2)
        rows = pl.ds(*PIECES[k])
        return pltpu.make_async_remote_copy(
            src_ref=RL.at[rows] if leg else RX.at[b, rows],
            dst_ref=RX.at[2 * xi + 1 - side, rows] if leg else RL.at[rows],
            send_sem=z_send.at[leg, k], recv_sem=z_recv.at[leg, k],
            device_id=(dd, bb), device_id_type=MESH,
        )

    for k in range(4):
        z_copy(0, k).start()
    x_copies = [whole_copy(b, p, x_send.at[j]) for j, p in enumerate(xpeers)]
    for c in x_copies:
        c.start()

    def exchange(step, down_src, down_dst, up_src, up_dst):
        down = node_copy(down_src, down_dst, 2 * step, d - 1)
        up = node_copy(up_src, up_dst, 2 * step + 1, d + 1)
        return down, up

    halo_down, halo_up = exchange(
        0, SX.at[pl.ds(LOW + FACE, FACE)], SX.at[pl.ds(HIGH + FACE, FACE)],
        SX.at[pl.ds(HIGH, FACE)], SX.at[pl.ds(LOW, FACE)],
    )
    sum_down, sum_up = exchange(
        1, T.at[pl.ds(LOW, 2 * FACE)], XR.at[1], T.at[pl.ds(HIGH, 2 * FACE)], XR.at[0]
    )
    own_down, own_up = exchange(
        2, T.at[pl.ds(LOW, FACE)], YR.at[1], T.at[pl.ds(HIGH + FACE, FACE)], YR.at[0]
    )

    loads[0].wait()
    loads[1].wait()

    @pl.when(has_low)
    def _():
        halo_down.start()

    @pl.when(has_high)
    def _():
        halo_up.start()

    CP[...] = jnp.full(CP.shape, -1, i32)
    load_conn.wait()
    n = CN[...]
    CP[:, 0:NPC] = jnp.where(n < 2 * FACE, n + LOW, jnp.where(n < OWN, n - 2 * FACE, n))

    def cell_of(s):
        side = s // nx
        return 2 * ((xi + s) % nx) + zh + side * (1 - 2 * zh)

    rows = [CP[pl.ds(cell_of(s), 1), :] for s in range(CELLS)]
    near = [r[:, :KC] for r in rows[:nx]]
    top = [r[:, :256] for r in rows[nx:]]
    bottom = [r[:, 256:KC] for r in rows[nx:]]
    CR[...] = jnp.concatenate(near + top + bottom, axis=1)

    def build_g(s, carry):
        line = jnp.broadcast_to(CP[pl.ds(cell_of(s), 1), :], (8, 384))
        column = jnp.transpose(line)[:KC, 0:1]
        wanted = jnp.broadcast_to(column, (KC, 128)).astype(i16)
        for j in range(EXT // 128):
            place = (lax.broadcasted_iota(i32, (KC, 128), 1) + j * 128).astype(i16)
            G[pl.ds(pl.multiple_of(s * KC, KC), KC), j * 128 : (j + 1) * 128] = jnp.where(
                wanted == place, bf16(1), bf16(0)
            )
        return carry

    lax.fori_loop(0, CELLS, build_g, 0)

    def build_s(j, carry):
        place = (lax.broadcasted_iota(i32, (256, 128), 0) + j * 256).astype(i16)
        for t in range(CELLS * KC // 128):
            wanted = jnp.broadcast_to(CR[0:1, t * 128 : (t + 1) * 128], (256, 128)).astype(i16)
            S[pl.ds(pl.multiple_of(j * 256, 256), 256), t * 128 : (t + 1) * 128] = jnp.where(
                wanted == place, bf16(1), bf16(0)
            )
        return carry

    lax.fori_loop(0, EXT // 256, build_s, 0)

    loads[2].wait()

    @pl.when(has_low)
    def _():
        halo_up.wait_recv()

    @pl.when(jnp.logical_not(has_low))
    def _():
        SX[LOW : LOW + FACE] = jnp.zeros((FACE, COLS), f32)

    @pl.when(has_high)
    def _():
        halo_down.wait_recv()

    @pl.when(jnp.logical_not(has_high))
    def _():
        SX[HIGH + FACE : EXT] = jnp.zeros((FACE, COLS), f32)

    def set_field(at, count, value):
        hi, lo = split(value)
        E[at : at + count, 0:COLS] = hi
        E[at : at + count, COLS : 2 * COLS] = lo

    set_field(0, EXT, SX[...])

    half_rows = CELLS * KC // 2

    def gather_half(m, start, stop, first):
        r = pl.ds(pl.multiple_of(m * half_rows, half_rows), half_rows)
        got = jnp.dot(G[r, start:stop], E[start:stop], preferred_element_type=f32)
        if not first:
            got = got + X[r, :].astype(f32)
        X[r, :] = got.astype(bf16)

    def gather(start, stop, first):
        def body(m, carry):
            gather_half(m, start, stop, first)
            return carry

        lax.fori_loop(0, 2, body, 0)

    def relay(group):
        for k in (2 * group, 2 * group + 1):
            z_copy(0, k).wait_recv()
            z_copy(1, k).start()

    def forward(group):
        for k in (2 * group, 2 * group + 1):
            z_copy(1, k).wait_recv()
            for j, p in enumerate(xpeers):
                piece_copy(zpeer, k, p, f_send.at[k, j]).start()

    def put(s, at, count, lane, value):
        hi, lo = split(value)
        base, step = (at, 256) if at < 256 else (512 + at - 256, 96)
        Hs[s, base : base + count, lane : lane + 128] = hi
        Hs[s, base + step : base + step + count, lane : lane + 128] = lo

    def unpack_b(s, e):
        for i in range(2):
            part = RX[e, PB + 88 * i : PB + 88 * (i + 1)]
            if i == 0:
                part = jnp.where(row88 == 87, 0.0, part)
            put(s, 256, 96, 128 * i, padded(part, 96))
            put(s, 128 * i, 128, 256, jnp.transpose(padded(part, 128)))

    def unpack_a(s, e):
        part = RX[e, PA : PA + 128]
        put(s, 128, 128, 0, part)
        put(s, 0, 128, 128, jnp.transpose(part))

    def unpack_d(s, e):
        part = RX[e, PD : PD + 128]
        flipped = jnp.transpose(part)
        middle = RX[e, PB + 87 : PB + 88]
        put(s, 0, 128, 0, jnp.where(row >= col, part, flipped))
        put(s, 128, 128, 128, jnp.where(row < col, part, jnp.where(row > col, flipped, middle)))

    def unpack_c(s, e):
        put(s, 256, 96, 256, padded(unpack_corner(RX[e, PC : PC + 48], lane_roll), 96))

    TOPS = nx * KC
    BOTTOMS = TOPS + nx * 256

    def product(s, base, count, *parts):
        t = jnp.dot(
            Hs[s, base : base + count, :KC], X[s * KC : (s + 1) * KC], preferred_element_type=f32
        )
        for at, rows, to in parts:
            hi_part, lo_part = t[at : at + rows], t[at + rows : at + 2 * rows]
            p = (lo_part[:, COLS:] + lo_part[:, :COLS]) + (hi_part[:, COLS:] + hi_part[:, :COLS])
            hi, lo = split(p)
            PR[to : to + rows, 0:COLS] = hi
            PR[to : to + rows, COLS : 2 * COLS] = lo

    def near_products():
        for j in range(nx):
            product(j, 0, 704, (0, 256, j * KC), (512, 96, j * KC + 256))

    def far_tops(some):
        for j in some:
            product(nx + j, 0, 512, (0, 256, TOPS + j * 256))

    def far_bottoms():
        for j in range(nx):
            product(nx + j, 512, 192, (0, 96, BOTTOMS + j * 96))

    def far_products():
        for j in range(nx):
            product(nx + j, 0, 704, (0, 256, TOPS + j * 256), (512, 96, BOTTOMS + j * 96))

    def scatter(at, count, start, stop, first):
        w = pl.ds(at, count)
        got = jnp.dot(S[w, start:stop], PR[start:stop], preferred_element_type=f32)
        got = got[:, :COLS] + got[:, COLS:]
        T[w, :] = got if first else T[w, :] + got

    def near_cell(j, carry):
        e = cell_of(j)

        @pl.when(j > 0)
        def _():
            whole_copy(e, zpeer, x_send.at[0]).wait_recv()

        unpack_b(j, e)
        unpack_a(j, e)
        unpack_d(j, e)
        unpack_c(j, e)
        return carry

    far_cells = [cell_of(nx + j) for j in range(nx)]

    def arrived(group):
        for e in far_cells[1:]:
            for k in (2 * group, 2 * group + 1):
                piece_copy(e, k, zpeer, z_send.at[0, k]).wait_recv()

    core = d % 2
    down_first = core == 0

    def start_both(down, up):
        def begin(place):
            @pl.when(has_low & (down_first if place == 0 else jnp.logical_not(down_first)))
            def _():
                down.start()

            @pl.when(has_high & (jnp.logical_not(down_first) if place == 0 else down_first))
            def _():
                up.start()

        return begin

    end = BOTTOMS + nx * 96

    relay(0)
    z_copy(0, 4).start()
    z_copy(0, 5).start()
    gather_half(0, 0, EXT, True)
    gather_half(1, 0, EXT, True)
    relay(1)
    lax.fori_loop(0, nx, near_cell, 0)
    near_products()
    forward(0)
    relay(2)
    for at in range(0, EXT, EXT // 2):
        scatter(at, EXT // 2, 0, TOPS, True)
    forward(1)
    forward(2)
    arrived(0)
    for j, e in enumerate(far_cells):
        unpack_b(nx + j, e)
    arrived(1)
    for j, e in enumerate(far_cells):
        unpack_a(nx + j, e)
        unpack_c(nx + j, e)
    far_bottoms()
    for at in range(0, EXT, EXT // 2):
        scatter(at, EXT // 2, BOTTOMS, end, False)
    for some in ((0,), (1, 3), (2,)):
        for j in some:
            if j > 0:
                for k in (4, 5):
                    piece_copy(far_cells[j], k, zpeer, z_send.at[0, k]).wait_recv()
        for j in some:
            unpack_d(nx + j, far_cells[j])
        far_tops(some)
    begin_sums = start_both(sum_down, sum_up)
    for place in range(2):
        region = core if place == 0 else 1 - core
        scatter(pl.multiple_of(LOW + 2 * FACE * region, 2 * FACE), 2 * FACE, TOPS, BOTTOMS, False)
        begin_sums(place)
    scatter(0, INNER, TOPS, BOTTOMS, False)

    def keep_field(at, count, value):
        w = pl.ds(at, count)
        F[w, :] = value
        hi, lo = split(value)
        E[w, 0:COLS] = hi
        E[w, COLS : 2 * COLS] = lo

    def as_first(total, at, count):
        return (total - center * SX[pl.ds(at, count), :]) * (1.0 / half)

    keep_field(0, INNER, as_first(T[0:INNER], 0, INNER))
    gather(0, EARLY, True)

    def wait_for(region, from_low, from_high, buffer):
        low, high = region == 0, region == 1

        @pl.when(low & has_low)
        def _():
            from_low.wait_recv()

        @pl.when(high & has_high)
        def _():
            from_high.wait_recv()

        @pl.when((low & jnp.logical_not(has_low)) | (high & jnp.logical_not(has_high)))
        def _():
            buffer[region] = jnp.zeros(buffer.shape[1:], f32)

    for place in range(2):
        region = 1 - core if place == 0 else core
        wait_for(region, sum_up, sum_down, XR)
        for part in range(2):
            at = pl.multiple_of(LOW + 2 * FACE * region + FACE * part, FACE)
            total = T[pl.ds(at, FACE), :] + XR[region, FACE * part : FACE * (part + 1)]
            inside = (region == 1) | has_low if part == 0 else (region == 0) | has_high
            keep_field(at, FACE, jnp.where(inside, as_first(total, at, FACE), 0.0))
    gather(EARLY, EXT, False)

    near_products()
    far_products()

    @pl.when(has_low)
    def _():
        sum_down.wait_send()

    @pl.when(has_high)
    def _():
        sum_up.wait_send()

    begin_owned = start_both(own_down, own_up)
    for place in range(2):
        region = core if place == 0 else 1 - core
        scatter(pl.multiple_of(LOW + 3 * FACE * region, FACE), FACE, 0, end, True)
        begin_owned(place)

    def finish(i, to, at, count, total):
        part = pl.ds(to, count)
        out[part, :] = (total - center * F[pl.ds(at, count), :]) * (2.0 / half)

    scatter(0, INNER, 0, end, True)
    finish(0, FACE, 0, INNER, T[0:INNER])
    scatter(LOW + FACE, 2 * FACE, 0, end, True)
    for place in range(2):
        region = 1 - core if place == 0 else core
        wait_for(region, own_up, own_down, YR)
        at = pl.multiple_of(LOW + FACE + FACE * region, FACE)
        to = pl.multiple_of((OWN - FACE) * region, FACE)
        finish(1 + place, to, at, FACE, T[pl.ds(at, FACE), :] + YR[region])

    for c in x_copies:
        c.wait_send()
    for k in range(len(PIECES)):
        z_copy(0, k).wait_send()
        z_copy(1, k).wait_send()
        for j, p in enumerate(xpeers):
            piece_copy(zpeer, k, p, f_send.at[k, j]).wait_send()

    @pl.when(has_low)
    def _():
        halo_down.wait_send()
        own_down.wait_send()

    @pl.when(has_high)
    def _():
        halo_up.wait_send()
        own_up.wait_send()


def on_device(states, connectivity, cell_hamiltonian):
    anywhere = pl.BlockSpec(memory_space=pl.ANY)
    kt = CELLS * KC
    moved = pl.pallas_call(
        kernel,
        out_shape=pltpu.VMEM((OWN, COLS), f32),
        in_specs=[anywhere] * 3,
        out_specs=pl.BlockSpec(memory_space=pltpu.VMEM),
        scratch_shapes=[
            pltpu.VMEM((kt, EXT), bf16),
            pltpu.VMEM((EXT, kt), bf16),
            pltpu.VMEM((CELLS, 2 * KC, 384), bf16),
            pltpu.VMEM((kt, 2 * COLS), bf16),
            pltpu.VMEM((kt, 2 * COLS), bf16),
            pltpu.VMEM((EXT, 2 * COLS), bf16),
            pltpu.VMEM((CELLS, PROWS, 128), f32),
            pltpu.VMEM((EXT, COLS), f32),
            pltpu.VMEM((EXT, COLS), f32),
            pltpu.VMEM((EXT, COLS), f32),
            pltpu.VMEM((2, 2 * FACE, COLS), f32),
            pltpu.VMEM((2, FACE, COLS), f32),
            pltpu.VMEM((KC, 384), f32),
            pltpu.VMEM((CELLS, 384), i32),
            pltpu.VMEM((1, kt), i32),
            pltpu.VMEM((CELLS, NPC), i32),
            pltpu.VMEM((NPC, 1, NPC), f32),
            pltpu.VMEM((PROWS, 128), f32),
            pltpu.SemaphoreType.DMA((2, 6)),
            pltpu.SemaphoreType.DMA((2, 6)),
            pltpu.SemaphoreType.DMA((3,)),
            pltpu.SemaphoreType.DMA((6, 3)),
            pltpu.SemaphoreType.DMA((6,)),
            pltpu.SemaphoreType.DMA((CELLS, 6)),
            pltpu.SemaphoreType.DMA((6,)),
            pltpu.SemaphoreType.DMA((5,)),
        ],
        compiler_params=pltpu.CompilerParams(
            collective_id=0, has_side_effects=True, vmem_limit_bytes=58 << 20
        ),
    )(states, connectivity, cell_hamiltonian.reshape(NPC, 1, NPC))
    return moved - states


def solution(mesh):
    return jax.shard_map(
        on_device,
        mesh=mesh,
        in_specs=(P("domain", "band"), P("domain", None), P(("domain", "band"), None, None)),
        out_specs=P("domain", "band"),
        check_vma=False,
    )
```
